128 devices in a mesh: face: 8 (over y_lo, x), row: 16 (over y_hi, z, core).
Axes of the slice: x: 4, y: 4 (y_hi: 2, y_lo: 2; y = y_hi * 2 + y_lo), z: 4, core: 2. Of those that a mesh axis runs over, the one named last changes fastest.
Arguments:
- state_field: bfloat16 [8, 256, 256, 128], P('face', 'row'), may hold values from -6 to 6
- adjacency: int32 [2, 8, 4], replicated, may hold values from 0 to 7, as said below
- edge_flips: int32 [8, 2], replicated, may hold values from 0 to 1, as said below
- conv_first: bfloat16 [3, 3, 128, 128], replicated, may hold values from -0.1875 to 0.1875
- bias_first: float32 [128], replicated, may hold values from -3 to 3
- conv_second: bfloat16 [3, 3, 128, 128], replicated, may hold values from -0.1875 to 0.1875
- bias_second: float32 [128], replicated, may hold values from -3 to 3
- norm_gain: float32 [128], replicated, may hold values from 0.1 to 1.9
- up_weight: bfloat16 [128, 512], replicated, may hold values from -0.5 to 0.5
- up_bias: float32 [512], replicated, may hold values from -3 to 3
- down_weight: bfloat16 [512, 128], replicated, may hold values from -0.25 to 0.25
- down_bias: float32 [128], replicated, may hold values from -3 to 3
Outputs:
- block_out: bfloat16 [8, 256, 256, 128], P('face', 'row')
The draws below stay inside these ranges and needn't reach their ends.
Inputs may be any that keep to these rules, and one draw needn't show every extreme that they name: adjacency[0, f, e] is the face across edge e of face f and adjacency[1, f, e] the edge of that face that it meets; row edges (0, 1) meet row edges and column edges (2, 3) meet column edges; the pairing is mutual, every edge of every face in exactly one pair; column edges meet in the same order. `edge_flips`: equal for the two edges of a pair.
All inputs are finite; a program needn't handle non-finite values.
Results may differ from the reference program's by a relative error of at most 0.0045.
Values may be sent and summed in bfloat16 or wider, within the bound.
A program may use at most 64 MiB of HBM per device.

```python
import jax
import jax.numpy as jnp
from jax import lax

CHANNELS = 128
INNER = 512
NSIDE = 256
FACES = 8


def edge_matching(key, salt):
    item_count = 2 * FACES
    shuffled = jax.random.permutation(jax.random.fold_in(key, salt), item_count).astype(jnp.int32)
    position = jnp.argsort(shuffled, stable=True).astype(jnp.int32)
    partner = shuffled[jnp.bitwise_xor(position, 1)].astype(jnp.int32)
    return (position, partner)


def draw_adjacency(key, part):
    row_place, row_partner = edge_matching(key, 21)
    col_place, col_partner = edge_matching(key, 22)
    neighbours = jnp.concatenate([(row_partner // 2).reshape(FACES, 2), (col_partner // 2).reshape(FACES, 2)], 1)
    edge_sides = jnp.concatenate([(row_partner % 2).reshape(FACES, 2), (col_partner % 2 + 2).reshape(FACES, 2)], 1)
    return jnp.stack([neighbours, edge_sides]).astype(jnp.int32)


def draw_edge_flips(key, part):
    row_place, row_partner = edge_matching(key, 21)
    key = jax.random.fold_in(key, 5)
    pair_bits = jax.random.randint(key, (FACES,), 0, 2).astype(jnp.int32)
    pair_bits = pair_bits.at[0].set(1).at[1].set(0)
    return pair_bits[row_place // 2].reshape(FACES, 2).astype(jnp.int32)


def block_scale(stream_key, shape, pieces, low, top_value):
    factor_of, own = 1.0, jax.random.fold_in(stream_key, 6)
    for dim, blocks in pieces:
        heights = jnp.exp(jax.random.uniform(jax.random.fold_in(own, dim), (blocks,), jnp.float32, low / len(pieces), top_value / len(pieces)))
        factor_of = factor_of * jnp.repeat(heights, shape[dim] // blocks).reshape([-1 if axis == dim else 1 for axis in range(len(shape))])
    return factor_of


def centred(rng, extent, scale, bound, pieces=(), held_as=jnp.bfloat16):
    loudness = block_scale(rng, extent, pieces, -0.22, 0.18) if pieces else 1.0
    entries = jax.random.normal(rng, extent, jnp.float32) * scale * loudness
    return jnp.minimum(jnp.maximum(entries, -bound), bound).astype(held_as)


def setup_inputs(seed: int = 0) -> dict:
    splits = jax.random.split(jax.random.key(seed), 13)
    state_field = centred(splits[0], (FACES, NSIDE, NSIDE, CHANNELS), 1.0, 6.0, ((0, 8), (1, 16)))
    adjacency = draw_adjacency(jax.random.fold_in(splits[12], 71), 0)
    edge_flips = draw_edge_flips(jax.random.fold_in(splits[12], 71), 0)
    conv_first = centred(splits[3], (3, 3, CHANNELS, CHANNELS), (9 * CHANNELS) ** -0.5, 0.1875)
    bias_first = centred(splits[4], (CHANNELS,), 0.5, 3.0, (), jnp.float32)
    conv_second = centred(splits[5], (3, 3, CHANNELS, CHANNELS), (9 * CHANNELS) ** -0.5, 0.1875)
    bias_second = centred(splits[6], (CHANNELS,), 0.5, 3.0, (), jnp.float32)
    norm_gain = jnp.clip(1.0 + 0.18 * jax.random.normal(splits[7], (CHANNELS,), jnp.float32), 0.1, 1.9)
    up_weight = centred(splits[8], (CHANNELS, INNER), CHANNELS ** -0.5, 0.5)
    up_bias = centred(splits[9], (INNER,), 0.5, 3.0, (), jnp.float32)
    down_weight = centred(splits[10], (INNER, CHANNELS), INNER ** -0.5, 0.25)
    down_bias = centred(splits[11], (CHANNELS,), 0.5, 3.0, (), jnp.float32)
    return dict(state_field=state_field, adjacency=adjacency, edge_flips=edge_flips, conv_first=conv_first, bias_first=bias_first, conv_second=conv_second, bias_second=bias_second, norm_gain=norm_gain, up_weight=up_weight, up_bias=up_bias, down_weight=down_weight, down_bias=down_bias)


def gelu_exact(values):
    return jax.nn.gelu(values, approximate=False)

def convolve_padded(padded, kernel):
    row_count = padded.shape[0] - 2
    col_count = padded.shape[1] - 2
    chan_count = kernel.shape[3]
    summed = jnp.zeros((row_count * col_count, chan_count), jnp.float32)
    for row_step in range(3):
        for col_step in range(3):
            window = padded[row_step:row_step + row_count, col_step:col_step + col_count]
            window = window.reshape(row_count * col_count, -1)
            summed = summed + jnp.dot(window, kernel[row_step, col_step], preferred_element_type=jnp.float32)
    return summed.reshape(row_count, col_count, chan_count)

def mixer(second_sum, residual, norm_gain, up_weight, up_bias, down_weight, down_bias):
    row_count, col_count, chan_count = second_sum.shape
    pixels = row_count * col_count
    blocks = max(1, pixels // 4096)
    while pixels % blocks:
        blocks = blocks - 1
    flat_rows = second_sum.reshape(blocks, pixels // blocks, chan_count)
    flat_skip = residual.reshape(blocks, pixels // blocks, chan_count)

    def mix_block(members):
        block_rows, skip_rows = members
        centre = block_rows - lax.optimization_barrier(jnp.mean(block_rows, -1, keepdims=True))
        spread = lax.optimization_barrier(jnp.mean(centre * centre, -1, keepdims=True))
        normed = (centre * lax.rsqrt(spread + 1e-06) * norm_gain).astype(jnp.bfloat16)
        hidden_act = gelu_exact(jnp.dot(normed, up_weight, preferred_element_type=jnp.float32) + up_bias).astype(jnp.bfloat16)
        projected = jnp.dot(hidden_act, down_weight, preferred_element_type=jnp.float32) + down_bias
        return (skip_rows.astype(jnp.float32) + projected).astype(jnp.bfloat16)
    return lax.map(mix_block, (flat_rows, flat_skip)).reshape(row_count, col_count, chan_count)

def face_rims(whole_field, adjacency, edge_flips):
    row_edges = jnp.stack([whole_field[:, 0], whole_field[:, -1]], 1)
    col_edges = jnp.stack([whole_field[:, :, 0], whole_field[:, :, -1]], 1)
    neighbour = adjacency[0]
    edge_sides = adjacency[1]
    upper_rim = row_edges[neighbour[:, 0], edge_sides[:, 0]]
    lower_rim = row_edges[neighbour[:, 1], edge_sides[:, 1]]
    upper_rim = jnp.where(edge_flips[:, 0][:, None, None] == 1, upper_rim[:, ::-1], upper_rim)
    lower_rim = jnp.where(edge_flips[:, 1][:, None, None] == 1, lower_rim[:, ::-1], lower_rim)
    left_rim = col_edges[neighbour[:, 2], edge_sides[:, 2] - 2]
    right_rim = col_edges[neighbour[:, 3], edge_sides[:, 3] - 2]
    return (upper_rim, lower_rim, left_rim, right_rim)

def pad_face(face_block, upper_rim, lower_rim, left_rim, right_rim):
    chan_count = face_block.shape[-1]
    corner = jnp.zeros((1, chan_count), face_block.dtype)
    middle = jnp.concatenate([left_rim[:, None], face_block, right_rim[:, None]], 1)
    upper_row = jnp.concatenate([corner, upper_rim, corner], 0)
    lower_row = jnp.concatenate([corner, lower_rim, corner], 0)
    return jnp.concatenate([upper_row[None], middle, lower_row[None]], 0)

def reference(state_field, adjacency, edge_flips, conv_first, bias_first, conv_second, bias_second, norm_gain, up_weight, up_bias, down_weight, down_bias):
    rims_first = face_rims(state_field, adjacency, edge_flips)

    def first_layer(members):
        face_block, upper_rim, lower_rim, left_rim, right_rim = members
        summed = convolve_padded(pad_face(face_block, upper_rim, lower_rim, left_rim, right_rim), conv_first)
        return gelu_exact(summed + bias_first).astype(jnp.bfloat16)
    first_act = lax.map(first_layer, (state_field,) + rims_first)
    rims_second = face_rims(first_act, adjacency, edge_flips)

    def second_layer(members):
        face_block, residual, upper_rim, lower_rim, left_rim, right_rim = members
        summed = convolve_padded(pad_face(face_block, upper_rim, lower_rim, left_rim, right_rim), conv_second) + bias_second
        return mixer(summed, residual, norm_gain, up_weight, up_bias, down_weight, down_bias)
    return lax.map(second_layer, (first_act, state_field) + rims_second)
```

```python
import jax
import jax.numpy as jnp
from jax import lax
from jax.experimental import pallas as pl
from jax.experimental.pallas import tpu as pltpu
from jax.sharding import PartitionSpec as P

MESH = pl.DeviceIdType.MESH
bf16 = jnp.bfloat16
f32 = jnp.float32

NF = 8
NR = 16
R = 16
C = 256
CH = 128
K3 = 3 * CH
NH = 2 * NF
PIECE = C // NH
STRIP = 32
SOUT = 24


def dot(a, b):
    return jnp.dot(a, b, preferred_element_type=f32)


def gelu(v):
    return (0.5 * v) * (1.0 + lax.erf(v * 0.7071067811865476))


def put3(ref, row, v):
    zero = jnp.zeros((1, CH), bf16)
    ref[row, :, 0:CH] = jnp.concatenate([zero, v[:-1]], 0)
    ref[row, :, CH : 2 * CH] = v
    ref[row, :, 2 * CH : K3] = jnp.concatenate([v[1:], zero], 0)


def pick_row(tile, index):
    rows = lax.broadcasted_iota(jnp.int32, tile.shape, 0)
    return jnp.sum(jnp.where(rows == index, tile, 0.0), 0, keepdims=True)


def pair_weights(ref, w):
    zero = jnp.zeros((K3, CH), bf16)
    ref[0 : 3 * K3, 0:CH] = w
    ref[3 * K3 : 4 * K3, 0:CH] = zero
    ref[K3 : 4 * K3, CH : 2 * CH] = w
    ref[0:K3, CH : 2 * CH] = zero


def kernel(
    adj, flips, x, w1, b1, w2, b2, gain, wu, bu, wd, bd,
    out,
    X3, F3, T3, wp1, wp2, COL, HIN, PB, CBT, ST, SEL, SIN, EXT, XC, FS,
    colS, colR, rowS, rowR, pbS, pbR, cbS, cbR, stS, stR, selS, selR,
):
    f = lax.axis_index("face")
    r = lax.axis_index("row")
    top = r == 0
    bottom = r == NR - 1
    hot = jnp.logical_or(top, bottom)
    re = jnp.where(bottom, 1, 0)
    h = 2 * f + re

    def hot_device(m):
        return {"face": m // 2, "row": (m % 2) * (NR - 1)}

    barrier = pltpu.get_barrier_semaphore()

    def greet(device):
        pl.semaphore_signal(barrier, inc=1, device_id=device, device_id_type=MESH)

    @pl.loop(1, NF)
    def _(o):
        greet({"face": (f + o) % NF, "row": r})

    @pl.when(r > 0)
    def _():
        greet({"face": f, "row": r - 1})

    @pl.when(r < NR - 1)
    def _():
        greet({"face": f, "row": r + 1})

    @pl.when(hot)
    def _():
        @pl.loop(0, NF)
        def _(o):
            greet({"face": o, "row": (1 - re) * (NR - 1)})

    def column(c):
        base = (c // 16) * 16
        rows = [x[0, i, base : base + 16, :].astype(f32)[c - base : c - base + 1] for i in range(R)]
        return jnp.concatenate(rows, 0)

    own = [column(c) for c in (0, 1, C - 2, C - 1)]
    for k in range(4):
        COL[f, k] = own[k].astype(bf16)
        XC[k] = jnp.zeros((STRIP, CH), f32)
        XC[k, 2 : 2 + R, :] = own[k]

    @pl.when(hot)
    def _():
        firsts = jnp.concatenate([own[k][0:2] for k in range(4)] + [jnp.zeros((8, CH), f32)], 0)
        lasts = jnp.concatenate([own[k][R - 2 : R] for k in range(4)] + [jnp.zeros((8, CH), f32)], 0)
        CBT[h] = jnp.where(bottom, lasts, firsts).astype(bf16)
        PB[h] = x[0, pl.ds(re * (R - 2), 2), pl.ds(pl.multiple_of(h * PIECE, PIECE), PIECE), :]

    @pl.when(hot)
    def _():
        pl.semaphore_wait(barrier, 2 * NF)

    @pl.when(jnp.logical_not(hot))
    def _():
        pl.semaphore_wait(barrier, NF + 1)

    def col_copy(o, slot):
        return pltpu.make_async_remote_copy(
            src_ref=COL.at[slot], dst_ref=COL.at[slot],
            send_sem=colS.at[o], recv_sem=colR.at[slot],
            device_id={"face": (f + o) % NF, "row": r}, device_id_type=MESH,
        )

    def row_copy(d):
        return pltpu.make_async_remote_copy(
            src_ref=x.at[0, pl.ds((1 - d) * (R - 2), 2)], dst_ref=HIN.at[d],
            send_sem=rowS.at[d], recv_sem=rowR.at[d],
            device_id={"face": f, "row": r + 1 - 2 * d}, device_id_type=MESH,
        )

    def piece_copy(m, slot):
        return pltpu.make_async_remote_copy(
            src_ref=x.at[0, pl.ds(re * (R - 2), 2), pl.ds(pl.multiple_of(m * PIECE, PIECE), PIECE)],
            dst_ref=PB.at[slot],
            send_sem=pbS.at[m], recv_sem=pbR.at[slot],
            device_id=hot_device(m), device_id_type=MESH,
        )

    def corner_copy(m, slot):
        return pltpu.make_async_remote_copy(
            src_ref=CBT.at[slot], dst_ref=CBT.at[slot],
            send_sem=cbS.at[m], recv_sem=cbR.at[slot],
            device_id=hot_device(m), device_id_type=MESH,
        )

    @pl.when(hot)
    def _():
        @pl.loop(1, NH)
        def _(o):
            m = (h + o) % NH
            piece_copy(m, h).start()
            corner_copy(m, h).start()

    @pl.loop(1, NF)
    def _(o):
        col_copy(o, f).start()

    @pl.when(r < NR - 1)
    def _():
        row_copy(0).start()

    @pl.when(r > 0)
    def _():
        row_copy(1).start()

    pair_weights(wp1, w1[...])
    pair_weights(wp2, w2[...])
    bias1 = b1[...]
    bias2 = b2[...]
    norm_gain = gain[...]
    bias_up = bu[...]
    bias_down = bd[...]

    @pl.loop(0, R)
    def _(i):
        put3(X3, i + 2, x[0, i])

    def conv1_pairs(k, count):
        lhs = jnp.concatenate(
            [jnp.concatenate([X3[k + 2 * q + t] for t in range(4)], 1) for q in range(count)], 0
        )
        y = dot(lhs, wp1[...])
        for q in range(count):
            for j in range(2):
                v = y[C * q : C * (q + 1), CH * j : CH * (j + 1)]
                put3(F3, k + 2 * q + j, gelu(v + bias1).astype(bf16))

    @pl.loop(0, 3)
    def _(g):
        conv1_pairs(2 + 4 * g, 2)

    conv1_pairs(14, 1)

    @pl.loop(1, NF)
    def _(o):
        col_copy(o, (f + NF - o) % NF).wait_recv()

    fl, el = adj[0, f, 2], adj[1, f, 2] % 2
    fr, er = adj[0, f, 3], adj[1, f, 3] % 2
    SEL[0] = COL[fl, 3 * el]
    SEL[1] = COL[fl, 1 + el]
    SEL[2] = COL[fr, 3 * er]
    SEL[3] = COL[fr, 1 + er]

    def sel_copy(d):
        return pltpu.make_async_remote_copy(
            src_ref=SEL, dst_ref=SIN.at[d],
            send_sem=selS.at[d], recv_sem=selR.at[d],
            device_id={"face": f, "row": r + 1 - 2 * d}, device_id_type=MESH,
        )

    def chosen_copy(m, slot):
        return pltpu.make_async_remote_copy(
            src_ref=ST.at[m],
            dst_ref=HIN.at[m % 2, pl.ds(0, 2), pl.ds(pl.multiple_of(slot * PIECE, PIECE), PIECE)],
            send_sem=stS.at[m], recv_sem=stR.at[slot],
            device_id=hot_device(m), device_id_type=MESH,
        )

    @pl.when(r < NR - 1)
    def _():
        sel_copy(0).start()

    @pl.when(r > 0)
    def _():
        sel_copy(1).start()

    @pl.when(hot)
    def _():
        @pl.loop(1, NH)
        def _(o):
            piece_copy((h + o) % NH, (h + NH - o) % NH).wait_recv()

        @pl.loop(1, NH)
        def _(o):
            m = (h + o) % NH
            ST[m] = PB[2 * adj[0, m // 2, m % 2] + adj[1, m // 2, m % 2]]
            chosen_copy(m, h).start()

        HIN[re, :, pl.ds(pl.multiple_of(h * PIECE, PIECE), PIECE), :] = PB[
            2 * adj[0, f, re] + adj[1, f, re]
        ]

        @pl.loop(1, NH)
        def _(o):
            corner_copy((h + o) % NH, (h + NH - o) % NH).wait_recv()

    def mix(second, skip):
        second = second - jnp.mean(second, -1, keepdims=True)
        spread = jnp.mean(second * second, -1, keepdims=True)
        normed = (second * lax.rsqrt(spread + 1e-6) * norm_gain).astype(bf16)
        hidden = gelu(dot(normed, wu[...]) + bias_up).astype(bf16)
        return (skip.astype(f32) + (dot(hidden, wd[...]) + bias_down)).astype(bf16)

    @pl.loop(0, 3)
    def _(g):
        lhs = jnp.concatenate(
            [
                jnp.concatenate([F3[2 + 4 * g + 2 * q + t, 16 : C - 16, :] for t in range(4)], 1)
                for q in range(2)
            ],
            0,
        )
        y = dot(lhs, wp2[...])
        n = C - 32
        for q in range(2):
            for j in range(2):
                row = 2 + 4 * g + 2 * q + j
                second = y[n * q : n * (q + 1), CH * j : CH * (j + 1)] + bias2
                out[0, row, 16 : C - 16, :] = mix(second, x[0, row, 16 : C - 16, :])

    @pl.when(r > 0)
    def _():
        sel_copy(0).wait_recv()

    @pl.when(r < NR - 1)
    def _():
        sel_copy(1).wait_recv()

    @pl.when(r > 0)
    def _():
        row_copy(0).wait_recv()

    @pl.when(r < NR - 1)
    def _():
        row_copy(1).wait_recv()

    @pl.when(hot)
    def _():
        @pl.loop(1, NH)
        def _(o):
            chosen_copy((h + o) % NH, (h + NH - o) % NH).wait_recv()

    for k in range(4):
        EXT[k] = jnp.zeros((STRIP, CH), f32)
        EXT[k, 2 : 2 + R, :] = SEL[k].astype(f32)

    @pl.when(r > 0)
    def _():
        for k in range(4):
            EXT[k, 0:2, :] = SIN[0, k].astype(f32)[R - 2 : R]
        for j in range(2):
            XC[0, j : j + 1, :] = HIN[0, j, 0:16, :].astype(f32)[0:1]
            XC[3, j : j + 1, :] = HIN[0, j, C - 16 : C, :].astype(f32)[15:16]
            put3(X3, j, HIN[0, j])

    @pl.when(r < NR - 1)
    def _():
        for k in range(4):
            EXT[k, R + 2 : R + 4, :] = SIN[1, k].astype(f32)[0:2]
        for j in range(2):
            XC[0, R + 2 + j : R + 3 + j, :] = HIN[1, j, 0:16, :].astype(f32)[0:1]
            XC[3, R + 2 + j : R + 3 + j, :] = HIN[1, j, C - 16 : C, :].astype(f32)[15:16]
            put3(X3, R + 2 + j, HIN[1, j])

    def patch(ref, row, first, lanes, value, at):
        cells = ref[row, first : first + 16, lanes * CH : (lanes + 1) * CH].astype(f32)
        rows = lax.broadcasted_iota(jnp.int32, (16, CH), 0)
        ref[row, first : first + 16, lanes * CH : (lanes + 1) * CH] = jnp.where(
            rows == at, value, cells
        ).astype(bf16)

    def across(s):
        fu, eu = adj[0, f, s], adj[1, f, s]
        flip = flips[f, s]
        rows = lax.broadcasted_iota(jnp.int32, (C, C), 0)
        cols = lax.broadcasted_iota(jnp.int32, (C, C), 1)
        order = jnp.where(cols == jnp.where(flip == 1, C - 1 - rows, rows), 1.0, 0.0).astype(bf16)
        near = HIN[s, 0].astype(f32), HIN[s, 1].astype(f32)
        edge = jnp.where(eu == 1, near[1], near[0]).astype(bf16)
        turned = dot(order, jnp.concatenate([x[0, (R - 1) * s], edge], 1))
        mine = turned[:, 0:CH]
        put3(X3, 1 + (R + 1) * s, turned[:, CH : 2 * CH].astype(bf16))
        for t, v in enumerate(
            (
                jnp.where(eu == 1, near[0], mine),
                jnp.where(eu == 1, near[1], near[0]),
                jnp.where(eu == 1, mine, near[1]),
            )
        ):
            put3(T3, t, v.astype(bf16))
        for e in range(2):
            g, ge = adj[0, fu, 2 + e], adj[1, fu, 2 + e] % 2
            corner = CBT[2 * g + eu].astype(f32)
            cells = [pick_row(corner, 6 * ge + j) for j in range(2)]
            none = jnp.zeros((1, CH), f32)
            rim = (
                jnp.where(eu == 1, cells[0], none),
                jnp.where(eu == 1, cells[1], cells[0]),
                jnp.where(eu == 1, none, cells[1]),
            )
            for t in range(3):
                patch(T3, t, (C - 16) * e, 2 * e, rim[t], 15 * e)
        lhs = jnp.concatenate(
            [
                jnp.concatenate([T3[t] for t in range(3)], 1),
                jnp.concatenate([X3[1 + (R - 1) * s + t] for t in range(3)], 1),
            ],
            0,
        )
        y = gelu(dot(lhs, w1[...]) + bias1).astype(bf16)
        put3(F3, (R + 1) * s, dot(order, y[0:C]).astype(bf16))
        put3(F3, 1 + (R - 1) * s, y[C : 2 * C])

    @pl.loop(0, R + 4)
    def _(k):
        patch(X3, k, 0, 0, EXT[0, pl.ds(k, 1), :], 0)
        patch(X3, k, C - 16, 2, EXT[2, pl.ds(k, 1), :], 15)

    for s in range(2):
        is_end = (top, bottom)[s]

        @pl.when(jnp.logical_not(is_end))
        def _():
            conv1_pairs(R * s, 1)

        @pl.when(is_end)
        def _():
            across(s)
            for e in range(2):
                g0, e0 = adj[0, f, 2 + e], adj[1, f, 2 + e] % 2
                g, ge, turn = adj[0, g0, s], adj[1, g0, s], flips[g0, s]
                corner = CBT[2 * g + ge].astype(f32)
                for depth in range(2):
                    at = 3 * e0 if depth == 0 else 1 + e0
                    at = jnp.where(turn == 1, 3 - at, at)
                    EXT[2 * e + depth, 1 + (R + 1) * s : 2 + (R + 1) * s, :] = pick_row(
                        corner, 2 * at + ge
                    )

    def taps(columns):
        return jnp.concatenate(
            [v[a : a + SOUT] for a in range(3) for v in columns], 1
        ).astype(bf16)

    l0, l1, r0, r1 = EXT[0], EXT[1], EXT[2], EXT[3]
    x0, x1, x2, x3 = XC[0], XC[1], XC[2], XC[3]
    lhs = jnp.concatenate(
        [
            taps((jnp.where(el == 1, l1, x0), l0, jnp.where(el == 1, x0, l1))),
            taps((l0, x0, x1)),
            taps((x2, x3, r0)),
            taps((jnp.where(er == 1, r1, x3), r0, jnp.where(er == 1, x3, r1))),
        ],
        0,
    )
    strips = gelu(dot(lhs, w1[...]) + bias1)
    for k in range(4):
        FS[k] = strips[SOUT * k : SOUT * (k + 1)]

    for s in range(2):

        @pl.when((top, bottom)[s])
        def _():
            for k in (0, 3):
                FS[k, (R + 1) * s : (R + 1) * s + 1, :] = jnp.zeros((1, CH), f32)

    @pl.loop(0, R + 2)
    def _(k):
        patch(F3, k, 0, 0, FS[0, pl.ds(k, 1), :], 0)
        patch(F3, k, C - 16, 2, FS[3, pl.ds(k, 1), :], 15)

    @pl.loop(2, R)
    def _(k):
        v = FS[1, pl.ds(k, 1), :]
        patch(F3, k, 0, 1, v, 0)
        patch(F3, k, 0, 0, v, 1)
        v = FS[2, pl.ds(k, 1), :]
        patch(F3, k, C - 16, 1, v, 15)
        patch(F3, k, C - 16, 2, v, 14)

    @pl.loop(0, 2)
    def _(s):
        k = (R - 2) * s
        y = dot(jnp.concatenate([F3[k + t] for t in range(4)], 1), wp2[...])
        for j in range(2):
            second = y[:, CH * j : CH * (j + 1)] + bias2
            out[0, k + j] = mix(second, x[0, k + j])

    places = [(2 + 2 * q, 16 * (C // 16 - 1) * e) for q in range(R // 2 - 2) for e in range(2)]
    lhs = jnp.concatenate(
        [
            jnp.concatenate([F3[k + t, c : c + 16, :] for t in range(4)], 1)
            for k, c in places
        ],
        0,
    )
    y = dot(lhs, wp2[...])
    for j in range(2):
        skip = jnp.concatenate([x[0, k + j, c : c + 16, :] for k, c in places], 0)
        mixed = mix(y[:, CH * j : CH * (j + 1)] + bias2, skip)
        for i, (k, c) in enumerate(places):
            out[0, k + j, c : c + 16, :] = mixed[16 * i : 16 * (i + 1)]

    @pl.loop(1, NF)
    def _(o):
        col_copy(o, f).wait_send()

    @pl.when(r < NR - 1)
    def _():
        row_copy(0).wait_send()
        sel_copy(0).wait_send()

    @pl.when(r > 0)
    def _():
        row_copy(1).wait_send()
        sel_copy(1).wait_send()

    @pl.when(hot)
    def _():
        @pl.loop(1, NH)
        def _(o):
            m = (h + o) % NH
            piece_copy(m, h).wait_send()
            corner_copy(m, h).wait_send()
            chosen_copy(m, h).wait_send()


def per_device(
    state_field, adjacency, edge_flips, conv_first, bias_first, conv_second, bias_second,
    norm_gain, up_weight, up_bias, down_weight, down_bias,
):
    vmem = pl.BlockSpec(memory_space=pltpu.VMEM)
    smem = pl.BlockSpec(memory_space=pltpu.SMEM)
    dma = pltpu.SemaphoreType.DMA
    return pl.pallas_call(
        kernel,
        out_shape=jax.ShapeDtypeStruct((1, R, C, CH), bf16),
        in_specs=[smem, smem] + [vmem] * 10,
        out_specs=vmem,
        scratch_shapes=[
            pltpu.VMEM((R + 4, C, K3), bf16),
            pltpu.VMEM((R + 2, C, K3), bf16),
            pltpu.VMEM((3, C, K3), bf16),
            pltpu.VMEM((4 * K3, 2 * CH), bf16),
            pltpu.VMEM((4 * K3, 2 * CH), bf16),
            pltpu.VMEM((NF, 4, R, CH), bf16),
            pltpu.VMEM((2, 2, C, CH), bf16),
            pltpu.VMEM((NH, 2, PIECE, CH), bf16),
            pltpu.VMEM((NH, 16, CH), bf16),
            pltpu.VMEM((NH, 2, PIECE, CH), bf16),
            pltpu.VMEM((4, R, CH), bf16),
            pltpu.VMEM((2, 4, R, CH), bf16),
            pltpu.VMEM((4, STRIP, CH), f32),
            pltpu.VMEM((4, STRIP, CH), f32),
            pltpu.VMEM((4, SOUT, CH), f32),
            dma((NF,)), dma((NF,)), dma((2,)), dma((2,)),
            dma((NH,)), dma((NH,)), dma((NH,)), dma((NH,)), dma((NH,)), dma((NH,)),
            dma((2,)), dma((2,)),
        ],
        compiler_params=pltpu.CompilerParams(
            collective_id=0, has_side_effects=True, vmem_limit_bytes=56 << 20
        ),
        cost_estimate=pl.CostEstimate(flops=3_500_000_000, bytes_accessed=3_000_000, transcendentals=2_600_000),
    )(
        adjacency, edge_flips, state_field,
        conv_first.reshape(9 * CH, CH), bias_first.reshape(1, CH),
        conv_second.reshape(9 * CH, CH), bias_second.reshape(1, CH),
        norm_gain.reshape(1, CH), up_weight, up_bias.reshape(1, -1),
        down_weight, down_bias.reshape(1, CH),
    )


def solution(mesh):
    in_specs = (P("face", "row", None, None), P(), P(), P(), P(), P(), P(), P(), P(), P(), P(), P())
    out_specs = P("face", "row", None, None)
    return jax.shard_map(
        per_device, mesh=mesh, in_specs=in_specs, out_specs=out_specs, check_vma=False
    )
```

```python
import jax
import jax.numpy as jnp
from jax import lax
from jax.experimental import pallas as pl
from jax.experimental.pallas import tpu as pltpu
from jax.sharding import PartitionSpec as P

MESH = pl.DeviceIdType.MESH
bf16 = jnp.bfloat16
f32 = jnp.float32

NF = 8
NR = 16
R = 16
C = 256
CH = 128
K3 = 3 * CH
NH = 2 * NF
PIECE = C // NF
STRIP = 32
SOUT = 24


def dot(a, b):
    return jnp.dot(a, b, preferred_element_type=f32)


def gelu(v):
    return (0.5 * v) * (1.0 + lax.erf(v * 0.7071067811865476))


def put3(ref, row, v):
    zero = jnp.zeros((1, CH), bf16)
    ref[row, :, 0:CH] = jnp.concatenate([zero, v[:-1]], 0)
    ref[row, :, CH : 2 * CH] = v
    ref[row, :, 2 * CH : K3] = jnp.concatenate([v[1:], zero], 0)


def kernel(
    adj, flips, x_hbm, w1_hbm, b1, w2_hbm, b2, gain, wu_hbm, bu, wd_hbm, bd,
    out,
    x, wp1, wp2, wu, wd, X3, F3, T3, COL, HIN, PB, CT, CTB, ST, SEL, SIN, EXT, XC, FS,
    locS, colS, colR, rowS, rowR, pbS, pbR, ctS, ctR, stS, stR, selS, selR,
):
    f = lax.axis_index("face")
    r = lax.axis_index("row")
    top = r == 0
    bottom = r == NR - 1
    hot = jnp.logical_or(top, bottom)
    middle = r == 1
    re = jnp.where(bottom, 1, 0)
    h = 2 * f + re
    place = f % 4

    def hot_device(m):
        return {"face": m // 2, "row": (m % 2) * (NR - 1)}

    local = [
        pltpu.make_async_copy(src, dst, locS.at[i])
        for i, (src, dst) in enumerate(
            (
                (x_hbm.at[0], x),
                (w1_hbm, wp1.at[pl.ds(0, 3 * K3), pl.ds(0, CH)]),
                (w1_hbm, wp1.at[pl.ds(K3, 3 * K3), pl.ds(CH, CH)]),
                (w2_hbm, wp2.at[pl.ds(0, 3 * K3), pl.ds(0, CH)]),
                (w2_hbm, wp2.at[pl.ds(K3, 3 * K3), pl.ds(CH, CH)]),
                (wu_hbm, wu),
                (wd_hbm, wd),
            )
        )
    ]
    for copy in local:
        copy.start()

    barrier = pltpu.get_barrier_semaphore()

    def greet(device):
        pl.semaphore_signal(barrier, inc=1, device_id=device, device_id_type=MESH)

    @pl.when(middle)
    def _():
        @pl.loop(0, NF)
        def _(o):
            greet({"face": o, "row": NR - 1})

        @pl.loop(0, NF)
        def _(o):
            greet({"face": o, "row": 0})

    @pl.loop(1, NF)
    def _(o):
        greet({"face": (f + o) % NF, "row": r})

    @pl.when(r > 0)
    def _():
        greet({"face": f, "row": r - 1})

    @pl.when(r < NR - 1)
    def _():
        greet({"face": f, "row": r + 1})

    def col_copy(o, slot):
        return pltpu.make_async_remote_copy(
            src_ref=COL.at[slot], dst_ref=COL.at[slot],
            send_sem=colS.at[o], recv_sem=colR.at[slot],
            device_id={"face": (f + o) % NF, "row": r}, device_id_type=MESH,
        )

    def row_copy(d):
        return pltpu.make_async_remote_copy(
            src_ref=x_hbm.at[0, pl.ds((1 - d) * (R - 2), 2)], dst_ref=HIN.at[d],
            send_sem=rowS.at[d], recv_sem=rowR.at[d],
            device_id={"face": f, "row": r + 1 - 2 * d}, device_id_type=MESH,
        )

    def piece_copy(m, slot):
        return pltpu.make_async_remote_copy(
            src_ref=x_hbm.at[
                0, pl.ds(re * (R - 2), 2), pl.ds(pl.multiple_of(m * PIECE, PIECE), PIECE)
            ],
            dst_ref=PB.at[slot],
            send_sem=pbS.at[m], recv_sem=pbR.at[slot],
            device_id={"face": m, "row": 1}, device_id_type=MESH,
        )

    def send_first():
        @pl.when(hot)
        def _():
            pl.semaphore_wait(barrier, 2 * NF)

            @pl.loop(0, NF)
            def _(o):
                piece_copy((f + o) % NF, h).start()

        @pl.when(jnp.logical_not(hot))
        def _():
            pl.semaphore_wait(barrier, NF + 1)

        @pl.loop(1, NF)
        def _(o):
            col_copy(o, f).start()

        @pl.when(r < NR - 1)
        def _():
            row_copy(0).start()

        @pl.when(r > 0)
        def _():
            row_copy(1).start()

    zero = jnp.zeros((K3, CH), bf16)
    for ref in (wp1, wp2):
        ref[3 * K3 : 4 * K3, 0:CH] = zero
        ref[0:K3, CH : 2 * CH] = zero
    bias1 = b1[...]
    bias2 = b2[...]
    norm_gain = gain[...]
    bias_up = bu[...]
    bias_down = bd[...]
    local[0].wait()

    def column(c):
        base = (c // 16) * 16
        rows = [x[i, base : base + 16, :].astype(f32)[c - base : c - base + 1] for i in range(R)]
        return jnp.concatenate(rows, 0)

    for k, c in enumerate((0, 1, C - 2, C - 1)):
        own = column(c)
        COL[f, k] = own.astype(bf16)
        XC[k] = jnp.zeros((STRIP, CH), f32)
        XC[k, 2 : 2 + R, :] = own

    @pl.when(bottom)
    def _():
        send_first()

    @pl.loop(0, R)
    def _(i):
        put3(X3, i + 2, x[i])

    def conv1_pairs(k, count):
        lhs = jnp.concatenate(
            [jnp.concatenate([X3[k + 2 * q + t] for t in range(4)], 1) for q in range(count)], 0
        )
        y = dot(lhs, wp1[...])
        for q in range(count):
            for j in range(2):
                v = y[C * q : C * (q + 1), CH * j : CH * (j + 1)]
                put3(F3, k + 2 * q + j, gelu(v + bias1).astype(bf16))

    local[1].wait()
    local[2].wait()
    conv1_pairs(14, 1)

    @pl.loop(0, 3)
    def _(g):
        @pl.when(jnp.logical_and(g == jnp.minimum(3 - place, 2), jnp.logical_not(bottom)))
        def _():
            send_first()

        conv1_pairs(2 + 4 * g, 2)

    for copy in local[3:]:
        copy.wait()

    fl, el = adj[0, 2, f], adj[1, 2, f] % 2
    fr, er = adj[0, 3, f], adj[1, 3, f] % 2

    def sel_copy(d):
        return pltpu.make_async_remote_copy(
            src_ref=SEL, dst_ref=SIN.at[d],
            send_sem=selS.at[d], recv_sem=selR.at[d],
            device_id={"face": f, "row": r + 1 - 2 * d}, device_id_type=MESH,
        )

    def send_strips():
        @pl.loop(1, NF)
        def _(o):
            col_copy(o, (f + NF - o) % NF).wait_recv()

        SEL[0] = COL[fl, 3 * el]
        SEL[1] = COL[fl, 1 + el]
        SEL[2] = COL[fr, 3 * er]
        SEL[3] = COL[fr, 1 + er]

        @pl.when(r < NR - 1)
        def _():
            sel_copy(0).start()

        @pl.when(r > 0)
        def _():
            sel_copy(1).start()

    def chosen_copy(m, slot):
        return pltpu.make_async_remote_copy(
            src_ref=ST.at[m],
            dst_ref=HIN.at[m % 2, pl.ds(0, 2), pl.ds(pl.multiple_of(slot * PIECE, PIECE), PIECE)],
            send_sem=stS.at[m], recv_sem=stR.at[slot],
            device_id=hot_device(m), device_id_type=MESH,
        )

    def corner_copy(m, side):
        return pltpu.make_async_remote_copy(
            src_ref=CT, dst_ref=CTB.at[side],
            send_sem=ctS.at[m], recv_sem=ctR.at[side],
            device_id=hot_device(m), device_id_type=MESH,
        )

    has_corner = jnp.logical_or(f == 0, f == NF - 1)
    side = jnp.where(f == 0, 0, 1)

    def order_of(o):
        return 2 * (o % NF) + o // NF

    def send_pieces():
        @pl.loop(0, NH)
        def _(m):
            pltpu.make_async_remote_copy(
                src_ref=ST.at[m], dst_ref=PB.at[m], send_sem=stS.at[m], recv_sem=pbR.at[m],
                device_id=hot_device(m), device_id_type=MESH,
            ).wait_recv()

        @pl.when(has_corner)
        def _():
            for g in range(NH // 4):
                cells = []
                for e in range(4 * g, 4 * g + 4):
                    for j in range(2):
                        first = PB[e, j, 0:16, :].astype(f32)[0:2]
                        last = PB[e, j, PIECE - 16 : PIECE, :].astype(f32)[14:16]
                        cells.append(jnp.where(f == 0, first, last))
                CT[g] = jnp.concatenate(cells, 0).astype(bf16)

        @pl.loop(0, NH)
        def _(o):
            m = order_of(o)
            ST[m] = PB[2 * adj[0, m % 2, m // 2] + adj[1, m % 2, m // 2]]
            chosen_copy(m, f).start()

            @pl.when(has_corner)
            def _():
                corner_copy(m, side).start()

    def mix(second, skip):
        second = second - jnp.mean(second, -1, keepdims=True)
        spread = jnp.mean(second * second, -1, keepdims=True)
        normed = (second * lax.rsqrt(spread + 1e-6) * norm_gain).astype(bf16)
        hidden = gelu(dot(normed, wu[...]) + bias_up).astype(bf16)
        return (skip.astype(f32) + (dot(hidden, wd[...]) + bias_down)).astype(bf16)

    @pl.loop(0, 3)
    def _(g):
        @pl.when(g == jnp.where(place == 0, 1, 0))
        def _():
            send_strips()

        @pl.when(jnp.logical_and(middle, jnp.logical_and(g == 2, place > 1)))
        def _():
            send_pieces()

        lhs = jnp.concatenate(
            [
                jnp.concatenate([F3[2 + 4 * g + 2 * q + t, 16 : C - 16, :] for t in range(4)], 1)
                for q in range(2)
            ],
            0,
        )
        y = dot(lhs, wp2[...])
        n = C - 32
        for q in range(2):
            for j in range(2):
                row = 2 + 4 * g + 2 * q + j
                second = y[n * q : n * (q + 1), CH * j : CH * (j + 1)] + bias2
                out[0, row, 16 : C - 16, :] = mix(second, x[row, 16 : C - 16, :])

    @pl.when(jnp.logical_and(middle, place <= 1))
    def _():
        send_pieces()

    @pl.when(r > 0)
    def _():
        sel_copy(0).wait_recv()
        row_copy(0).wait_recv()

    @pl.when(r < NR - 1)
    def _():
        sel_copy(1).wait_recv()
        row_copy(1).wait_recv()

    for k in range(4):
        EXT[k] = jnp.zeros((STRIP, CH), f32)
        EXT[k, 2 : 2 + R, :] = SEL[k].astype(f32)

    @pl.when(r > 0)
    def _():
        for k in range(4):
            EXT[k, 0:2, :] = SIN[0, k].astype(f32)[R - 2 : R]
        for j in range(2):
            XC[0, j : j + 1, :] = HIN[0, j, 0:16, :].astype(f32)[0:1]
            XC[3, j : j + 1, :] = HIN[0, j, C - 16 : C, :].astype(f32)[15:16]
            put3(X3, j, HIN[0, j])

    @pl.when(r < NR - 1)
    def _():
        for k in range(4):
            EXT[k, R + 2 : R + 4, :] = SIN[1, k].astype(f32)[0:2]
        for j in range(2):
            XC[0, R + 2 + j : R + 3 + j, :] = HIN[1, j, 0:16, :].astype(f32)[0:1]
            XC[3, R + 2 + j : R + 3 + j, :] = HIN[1, j, C - 16 : C, :].astype(f32)[15:16]
            put3(X3, R + 2 + j, HIN[1, j])

    def patch(ref, row, first, lanes, value, at):
        cells = ref[row, first : first + 16, lanes * CH : (lanes + 1) * CH].astype(f32)
        rows = lax.broadcasted_iota(jnp.int32, (16, CH), 0)
        ref[row, first : first + 16, lanes * CH : (lanes + 1) * CH] = jnp.where(
            rows == at, value, cells
        ).astype(bf16)

    @pl.loop(0, R + 4)
    def _(k):
        patch(X3, k, 0, 0, EXT[0, pl.ds(k, 1), :], 0)
        patch(X3, k, C - 16, 2, EXT[2, pl.ds(k, 1), :], 15)

    def taps(columns):
        return jnp.concatenate([v[a : a + v.shape[0] - 2] for a in range(3) for v in columns], 1)

    def outer_left(l0, l1, x0):
        return taps((jnp.where(el == 1, l1, x0), l0, jnp.where(el == 1, x0, l1)))

    def outer_right(r0, r1, x3):
        return taps((jnp.where(er == 1, r1, x3), r0, jnp.where(er == 1, x3, r1)))

    count = SOUT + 2
    lhs = jnp.concatenate(
        [
            outer_left(EXT[0, 0:count], EXT[1, 0:count], XC[0, 0:count]),
            taps((EXT[0, 0:count], XC[0, 0:count], XC[1, 0:count])),
            taps((XC[2, 0:count], XC[3, 0:count], EXT[2, 0:count])),
            outer_right(EXT[2, 0:count], EXT[3, 0:count], XC[3, 0:count]),
        ],
        0,
    )
    strips = gelu(dot(lhs.astype(bf16), wp1[0 : 3 * K3, 0:CH]) + bias1)
    for k in range(4):
        FS[k] = strips[SOUT * k : SOUT * (k + 1)]

    for s in range(2):

        @pl.when(jnp.logical_not((top, bottom)[s]))
        def _():
            conv1_pairs(R * s, 1)

    @pl.loop(0, R + 2)
    def _(k):
        patch(F3, k, 0, 0, FS[0, pl.ds(k, 1), :], 0)
        patch(F3, k, C - 16, 2, FS[3, pl.ds(k, 1), :], 15)

    @pl.loop(2, R)
    def _(k):
        v = FS[1, pl.ds(k, 1), :]
        patch(F3, k, 0, 1, v, 0)
        patch(F3, k, 0, 0, v, 1)
        v = FS[2, pl.ds(k, 1), :]
        patch(F3, k, C - 16, 1, v, 15)
        patch(F3, k, C - 16, 2, v, 14)

    def outer_rows(s):
        k = (R - 2) * s
        y = dot(jnp.concatenate([F3[k + t] for t in range(4)], 1), wp2[...])
        for j in range(2):
            second = y[:, CH * j : CH * (j + 1)] + bias2
            out[0, k + j] = mix(second, x[k + j])

    @pl.loop(0, 2)
    def _(s):
        @pl.when(jnp.logical_not(jnp.where(s == 0, top, bottom)))
        def _():
            outer_rows(s)

    places = [(2 + 2 * q, 16 * (C // 16 - 1) * e) for q in range(R // 2 - 2) for e in range(2)]
    lhs = jnp.concatenate(
        [
            jnp.concatenate([F3[k + t, c : c + 16, :] for t in range(4)], 1)
            for k, c in places
        ],
        0,
    )
    y = dot(lhs, wp2[...])
    for j in range(2):
        skip = jnp.concatenate([x[k + j, c : c + 16, :] for k, c in places], 0)
        mixed = mix(y[:, CH * j : CH * (j + 1)] + bias2, skip)
        for i, (k, c) in enumerate(places):
            out[0, k + j, c : c + 16, :] = mixed[16 * i : 16 * (i + 1)]

    def corner_cell(face, edge, j, at):
        e = 2 * face + edge
        tile = CTB[at // 2, e // 4].astype(f32)
        rows = lax.broadcasted_iota(jnp.int32, tile.shape, 0)
        return jnp.sum(
            jnp.where(rows == 4 * (e % 4) + 2 * j + at % 2, tile, 0.0), 0, keepdims=True
        )

    @pl.when(hot)
    def _():
        s = re

        @pl.loop(0, NF)
        def _(m):
            chosen_copy(h, m).wait_recv()

        for d in range(2):
            corner_copy(h, d).wait_recv()

        fu, eu = adj[0, s, f], adj[1, s, f]
        flip = flips[s, f]
        rows = lax.broadcasted_iota(jnp.int32, (C, C), 0)
        cols = lax.broadcasted_iota(jnp.int32, (C, C), 1)
        order = jnp.where(cols == jnp.where(flip == 1, C - 1 - rows, rows), 1.0, 0.0).astype(bf16)
        near = HIN[s, 0].astype(f32), HIN[s, 1].astype(f32)
        edge = jnp.where(eu == 1, near[1], near[0]).astype(bf16)
        turned = dot(order, jnp.concatenate([x[(R - 1) * s], edge], 1))
        mine = turned[:, 0:CH]
        put3(X3, 1 + (R + 1) * s, turned[:, CH : 2 * CH].astype(bf16))
        for t, v in enumerate(
            (
                jnp.where(eu == 1, near[0], mine),
                jnp.where(eu == 1, near[1], near[0]),
                jnp.where(eu == 1, mine, near[1]),
            )
        ):
            put3(T3, t, v.astype(bf16))
        none = jnp.zeros((1, CH), f32)
        for e in range(2):
            g, ge = adj[0, 2 + e, fu], adj[1, 2 + e, fu] % 2
            cells = [corner_cell(g, eu, j, 3 * ge) for j in range(2)]
            rim = (
                jnp.where(eu == 1, cells[0], none),
                jnp.where(eu == 1, cells[1], cells[0]),
                jnp.where(eu == 1, none, cells[1]),
            )
            for t in range(3):
                patch(T3, t, (C - 16) * e, 2 * e, rim[t], 15 * e)
            g0, e0 = adj[0, 2 + e, f], adj[1, 2 + e, f] % 2
            g, ge, turn = adj[0, s, g0], adj[1, s, g0], flips[s, g0]
            for depth in range(2):
                at = 3 * e0 if depth == 0 else 1 + e0
                at = jnp.where(turn == 1, 3 - at, at)
                EXT[2 * e + depth, pl.ds(1 + (R + 1) * s, 1), :] = corner_cell(g, ge, ge, at)

        near_rows = pl.ds(1 + (R - 1) * s, 10)
        strip = jnp.concatenate(
            [
                outer_left(EXT[0, near_rows], EXT[1, near_rows], XC[0, near_rows]),
                outer_right(EXT[2, near_rows], EXT[3, near_rows], XC[3, near_rows]),
            ],
            0,
        ).astype(bf16)
        lhs = jnp.concatenate(
            [
                jnp.concatenate([T3[t] for t in range(3)], 1),
                jnp.concatenate([X3[1 + (R - 1) * s + t] for t in range(3)], 1),
                strip,
            ],
            0,
        )
        y = gelu(dot(lhs, wp1[0 : 3 * K3, 0:CH]) + bias1)
        put3(F3, (R + 1) * s, dot(order, y[0:C].astype(bf16)).astype(bf16))
        put3(F3, 1 + (R - 1) * s, y[C : 2 * C].astype(bf16))
        patch(F3, 1 + (R - 1) * s, 0, 0, y[2 * C : 2 * C + 1], 0)
        patch(F3, 1 + (R - 1) * s, C - 16, 2, y[2 * C + 8 : 2 * C + 9], 15)
        outer_rows(s)

    @pl.loop(1, NF)
    def _(o):
        col_copy(o, f).wait_send()

    @pl.when(r < NR - 1)
    def _():
        row_copy(0).wait_send()
        sel_copy(0).wait_send()

    @pl.when(r > 0)
    def _():
        row_copy(1).wait_send()
        sel_copy(1).wait_send()

    @pl.when(hot)
    def _():
        @pl.loop(0, NF)
        def _(m):
            piece_copy(m, h).wait_send()

    @pl.when(middle)
    def _():
        @pl.loop(0, NH)
        def _(m):
            chosen_copy(m, f).wait_send()

            @pl.when(has_corner)
            def _():
                corner_copy(m, side).wait_send()


def per_device(
    state_field, adjacency, edge_flips, conv_first, bias_first, conv_second, bias_second,
    norm_gain, up_weight, up_bias, down_weight, down_bias,
):
    vmem = pl.BlockSpec(memory_space=pltpu.VMEM)
    smem = pl.BlockSpec(memory_space=pltpu.SMEM)
    hbm = pl.BlockSpec(memory_space=pl.ANY)
    dma = pltpu.SemaphoreType.DMA
    return pl.pallas_call(
        kernel,
        out_shape=jax.ShapeDtypeStruct((1, R, C, CH), bf16),
        in_specs=[smem, smem, hbm, hbm, vmem, hbm, vmem, vmem, hbm, vmem, hbm, vmem],
        out_specs=vmem,
        scratch_shapes=[
            pltpu.VMEM((R, C, CH), bf16),
            pltpu.VMEM((4 * K3, 2 * CH), bf16),
            pltpu.VMEM((4 * K3, 2 * CH), bf16),
            pltpu.VMEM(up_weight.shape, bf16),
            pltpu.VMEM(down_weight.shape, bf16),
            pltpu.VMEM((R + 4, C, K3), bf16),
            pltpu.VMEM((R + 2, C, K3), bf16),
            pltpu.VMEM((3, C, K3), bf16),
            pltpu.VMEM((NF, 4, R, CH), bf16),
            pltpu.VMEM((2, 2, C, CH), bf16),
            pltpu.VMEM((NH, 2, PIECE, CH), bf16),
            pltpu.VMEM((NH // 4, 16, CH), bf16),
            pltpu.VMEM((2, NH // 4, 16, CH), bf16),
            pltpu.VMEM((NH, 2, PIECE, CH), bf16),
            pltpu.VMEM((4, R, CH), bf16),
            pltpu.VMEM((2, 4, R, CH), bf16),
            pltpu.VMEM((4, STRIP, CH), f32),
            pltpu.VMEM((4, STRIP, CH), f32),
            pltpu.VMEM((4, SOUT, CH), f32),
            dma((7,)), dma((NF,)), dma((NF,)), dma((2,)), dma((2,)),
            dma((NF,)), dma((NH,)), dma((NH,)), dma((2,)), dma((NH,)), dma((NF,)),
            dma((2,)), dma((2,)),
        ],
        compiler_params=pltpu.CompilerParams(
            collective_id=0, has_side_effects=True, vmem_limit_bytes=56 << 20
        ),
        cost_estimate=pl.CostEstimate(
            flops=3_500_000_000, bytes_accessed=3_000_000, transcendentals=2_600_000
        ),
    )(
        jnp.transpose(adjacency, (0, 2, 1)), jnp.transpose(edge_flips), state_field,
        conv_first.reshape(9 * CH, CH), bias_first.reshape(1, CH),
        conv_second.reshape(9 * CH, CH), bias_second.reshape(1, CH),
        norm_gain.reshape(1, CH), up_weight, up_bias.reshape(1, -1),
        down_weight, down_bias.reshape(1, CH),
    )


def solution(mesh):
    in_specs = (P("face", "row", None, None), P(), P(), P(), P(), P(), P(), P(), P(), P(), P(), P())
    out_specs = P("face", "row", None, None)
    return jax.shard_map(
        per_device, mesh=mesh, in_specs=in_specs, out_specs=out_specs, check_vma=False
    )
```

```python
import jax
import jax.numpy as jnp
from jax import lax
from jax.experimental import pallas as pl
from jax.experimental.pallas import tpu as pltpu
from jax.sharding import PartitionSpec as P

MESH = pl.DeviceIdType.MESH
bf16 = jnp.bfloat16
f32 = jnp.float32

NF = 8
NR = 16
R = 16
C = 256
CH = 128
K3 = 3 * CH
NH = 2 * NF
PIECE = C // NF
STRIP = 32
SOUT = 24


def dot(a, b):
    return jnp.dot(a, b, preferred_element_type=f32)


def gelu(v):
    return (0.5 * v) * (1.0 + lax.erf(v * 0.7071067811865476))


def put3(ref, row, v):
    zero = jnp.zeros((1, CH), bf16)
    ref[row, :, 0:CH] = jnp.concatenate([zero, v[:-1]], 0)
    ref[row, :, CH : 2 * CH] = v
    ref[row, :, 2 * CH : K3] = jnp.concatenate([v[1:], zero], 0)


def kernel(
    adj, flips, x_hbm, w1_hbm, b1, w2_hbm, b2, gain, wu_hbm, bu, wd_hbm, bd,
    out,
    x, wp1, wp2, wu, wd, X3, F3, T3, NS, P15, COL, HIN, PB, CT, CTB, ST, SEL, SIN, EXT, XC, FS,
    locS, viaS, viaR, relS, colS, colR, rowS, rowR, pbS, pbR, ctS, ctR, stS, stR, selS, selR,
):
    f = lax.axis_index("face")
    r = lax.axis_index("row")
    top = r == 0
    bottom = r == NR - 1
    hot = jnp.logical_or(top, bottom)
    middle = r == 1
    relay = r == NR - 2
    re = jnp.where(bottom, 1, 0)
    h = 2 * f + re
    place = f % 4

    def hot_device(m):
        return {"face": m // 2, "row": (m % 2) * (NR - 1)}

    local = [
        pltpu.make_async_copy(src, dst, locS.at[i])
        for i, (src, dst) in enumerate(
            (
                (x_hbm.at[0], x),
                (w1_hbm, wp1.at[pl.ds(0, 3 * K3), pl.ds(0, CH)]),
                (w1_hbm, wp1.at[pl.ds(K3, 3 * K3), pl.ds(CH, CH)]),
                (w2_hbm, wp2.at[pl.ds(0, 3 * K3), pl.ds(0, CH)]),
                (w2_hbm, wp2.at[pl.ds(K3, 3 * K3), pl.ds(CH, CH)]),
                (wu_hbm, wu),
                (wd_hbm, wd),
            )
        )
    ]
    for copy in local:
        copy.start()

    barrier = pltpu.get_barrier_semaphore()

    def greet(device):
        pl.semaphore_signal(barrier, inc=1, device_id=device, device_id_type=MESH)

    @pl.when(middle)
    def _():
        @pl.loop(0, NF)
        def _(o):
            greet({"face": o, "row": NR - 1})

        @pl.loop(0, NF)
        def _(o):
            greet({"face": o, "row": 0})

    @pl.loop(1, NF)
    def _(o):
        greet({"face": (f + o) % NF, "row": jnp.where(bottom, NR - 2, r)})

    @pl.when(r > 0)
    def _():
        greet({"face": f, "row": r - 1})

    @pl.when(r < NR - 1)
    def _():
        greet({"face": f, "row": r + 1})

    def col_copy(o, slot):
        return pltpu.make_async_remote_copy(
            src_ref=COL.at[slot], dst_ref=COL.at[slot],
            send_sem=colS.at[o], recv_sem=colR.at[slot],
            device_id={"face": (f + o) % NF, "row": r}, device_id_type=MESH,
        )

    def row_copy(d):
        return pltpu.make_async_remote_copy(
            src_ref=x_hbm.at[0, pl.ds((1 - d) * (R - 2), 2)], dst_ref=HIN.at[d],
            send_sem=rowS.at[d], recv_sem=rowR.at[d],
            device_id={"face": f, "row": r + 1 - 2 * d}, device_id_type=MESH,
        )

    def piece_copy(m, slot):
        return pltpu.make_async_remote_copy(
            src_ref=x_hbm.at[
                0, pl.ds(re * (R - 2), 2), pl.ds(pl.multiple_of(m * PIECE, PIECE), PIECE)
            ],
            dst_ref=PB.at[slot],
            send_sem=pbS.at[m], recv_sem=pbR.at[slot],
            device_id={"face": m, "row": 1}, device_id_type=MESH,
        )

    def to_relay():
        return pltpu.make_async_remote_copy(
            src_ref=COL.at[f], dst_ref=P15, send_sem=viaS.at[0], recv_sem=viaR.at[0],
            device_id={"face": f, "row": NR - 2}, device_id_type=MESH,
        )

    def relay_copy(o):
        return pltpu.make_async_remote_copy(
            src_ref=P15, dst_ref=COL.at[f], send_sem=relS.at[o], recv_sem=colR.at[f],
            device_id={"face": (f + o) % NF, "row": NR - 1}, device_id_type=MESH,
        )

    def send_end_row():
        @pl.loop(0, NF)
        def _(o):
            piece_copy((f + o) % NF, h).start()

    def send_first():
        busy = jnp.logical_or(top, relay)

        @pl.when(busy)
        def _():
            pl.semaphore_wait(barrier, 2 * NF)

        @pl.when(jnp.logical_not(busy))
        def _():
            pl.semaphore_wait(barrier, NF + 1)

        @pl.loop(1, NF)
        def _(o):
            col_copy(o, f).start()

        @pl.when(top)
        def _():
            send_end_row()

        row_copy(0).start()

        @pl.when(r > 0)
        def _():
            row_copy(1).start()

        @pl.when(relay)
        def _():
            to_relay().wait_recv()

            @pl.loop(1, NF)
            def _(o):
                relay_copy(o).start()

    @pl.when(bottom)
    def _():
        pl.semaphore_wait(barrier, NF + 1)
        send_end_row()
        row_copy(1).start()

    zero = jnp.zeros((K3, CH), bf16)
    for ref in (wp1, wp2):
        ref[3 * K3 : 4 * K3, 0:CH] = zero
        ref[0:K3, CH : 2 * CH] = zero
    bias1 = b1[...]
    bias2 = b2[...]
    norm_gain = gain[...]
    bias_up = bu[...]
    bias_down = bd[...]
    local[0].wait()

    def column(c):
        base = (c // 16) * 16
        rows = [x[i, base : base + 16, :].astype(f32)[c - base : c - base + 1] for i in range(R)]
        return jnp.concatenate(rows, 0)

    for k, c in enumerate((0, 1, C - 2, C - 1)):
        own = column(c)
        COL[f, k] = own.astype(bf16)
        XC[k] = jnp.zeros((STRIP, CH), f32)
        XC[k, 2 : 2 + R, :] = own

    @pl.when(bottom)
    def _():
        to_relay().start()

    def send_at(point):
        @pl.when(jnp.logical_and(jnp.minimum(3 - place, 2) == point, jnp.logical_not(bottom)))
        def _():
            send_first()

    send_at(0)

    @pl.loop(0, R)
    def _(i):
        put3(X3, i + 2, x[i])

    def conv1_pairs(starts):
        lhs = jnp.concatenate(
            [jnp.concatenate([X3[k + t] for t in range(4)], 1) for k in starts], 0
        )
        y = dot(lhs, wp1[...])
        for q, k in enumerate(starts):
            for j in range(2):
                v = y[C * q : C * (q + 1), CH * j : CH * (j + 1)]
                put3(F3, k + j, gelu(v + bias1).astype(bf16))

    local[1].wait()
    local[2].wait()
    conv1_pairs(range(2, R, 2))
    send_at(1)

    for copy in local[3:]:
        copy.wait()

    def conv2_norm(segments):
        lhs = jnp.concatenate(
            [jnp.concatenate([F3[k + t, a:b, :] for t in range(4)], 1) for k, a, b in segments], 0
        )
        y = dot(lhs, wp2[...])
        parts, at = [], 0
        for k, a, b in segments:
            parts += [y[at : at + b - a, CH * j : CH * (j + 1)] for j in range(2)]
            at += b - a
        second = jnp.concatenate(parts, 0) + bias2
        second = second - jnp.mean(second, -1, keepdims=True)
        spread = jnp.mean(second * second, -1, keepdims=True)
        return (second * lax.rsqrt(spread + 1e-6) * norm_gain).astype(bf16)

    def pointwise(normed, skip):
        hidden = gelu(dot(normed, wu[...]) + bias_up).astype(bf16)
        return (skip.astype(f32) + (dot(hidden, wd[...]) + bias_down)).astype(bf16)

    def finish(segments):
        cells = [(k + j, a, b) for k, a, b in segments for j in range(2)]
        skip = jnp.concatenate([x[k, a:b, :] for k, a, b in cells], 0)
        mixed, at = pointwise(conv2_norm(segments), skip), 0
        for k, a, b in cells:
            out[0, k, a:b, :] = mixed[at : at + b - a]
            at += b - a

    fl, el = adj[0, 2, f], adj[1, 2, f] % 2
    fr, er = adj[0, 3, f], adj[1, 3, f] % 2

    def sel_copy(d):
        return pltpu.make_async_remote_copy(
            src_ref=SEL, dst_ref=SIN.at[d],
            send_sem=selS.at[d], recv_sem=selR.at[d],
            device_id={"face": f, "row": r + 1 - 2 * d}, device_id_type=MESH,
        )

    def send_strips():
        @pl.loop(1, NF)
        def _(o):
            col_copy(o, (f + NF - o) % NF).wait_recv()

        SEL[0] = COL[fl, 3 * el]
        SEL[1] = COL[fl, 1 + el]
        SEL[2] = COL[fr, 3 * er]
        SEL[3] = COL[fr, 1 + er]

        @pl.when(r < NR - 1)
        def _():
            sel_copy(0).start()

        @pl.when(r > 0)
        def _():
            sel_copy(1).start()

    def chosen_copy(m, slot):
        return pltpu.make_async_remote_copy(
            src_ref=ST.at[m],
            dst_ref=HIN.at[m % 2, pl.ds(0, 2), pl.ds(pl.multiple_of(slot * PIECE, PIECE), PIECE)],
            send_sem=stS.at[m], recv_sem=stR.at[slot],
            device_id=hot_device(m), device_id_type=MESH,
        )

    def corner_copy(m, side):
        return pltpu.make_async_remote_copy(
            src_ref=CT, dst_ref=CTB.at[side],
            send_sem=ctS.at[m], recv_sem=ctR.at[side],
            device_id=hot_device(m), device_id_type=MESH,
        )

    has_corner = jnp.logical_or(f == 0, f == NF - 1)
    side = jnp.where(f == 0, 0, 1)

    def order_of(o):
        return 2 * (o % NF) + o // NF

    def send_pieces():
        @pl.loop(0, NH)
        def _(m):
            pltpu.make_async_remote_copy(
                src_ref=ST.at[m], dst_ref=PB.at[m], send_sem=stS.at[m], recv_sem=pbR.at[m],
                device_id=hot_device(m), device_id_type=MESH,
            ).wait_recv()

        @pl.when(has_corner)
        def _():
            for g in range(NH // 4):
                cells = []
                for e in range(4 * g, 4 * g + 4):
                    for j in range(2):
                        first = PB[e, j, 0:16, :].astype(f32)[0:2]
                        last = PB[e, j, PIECE - 16 : PIECE, :].astype(f32)[14:16]
                        cells.append(jnp.where(f == 0, first, last))
                CT[g] = jnp.concatenate(cells, 0).astype(bf16)

        @pl.loop(0, NH)
        def _(o):
            m = order_of(o)
            ST[m] = PB[2 * adj[0, m % 2, m // 2] + adj[1, m % 2, m // 2]]
            chosen_copy(m, f).start()

            @pl.when(has_corner)
            def _():
                corner_copy(m, side).start()

    inner = C - 32
    normed = conv2_norm([(k, 16, C - 16) for k in range(2, R - 2, 2)])
    for i in range(R - 4):
        NS[i] = normed[inner * i : inner * (i + 1)]
    send_at(2)

    @pl.loop(0, 2)
    def _(g):
        rows = [(R // 2 - 2) * g + i for i in range(R // 2 - 2)]
        skip = jnp.concatenate([x[2 + i, 16 : C - 16, :] for i in rows], 0)
        mixed = pointwise(jnp.concatenate([NS[i] for i in rows], 0), skip)
        for q, i in enumerate(rows):
            out[0, 2 + i, 16 : C - 16, :] = mixed[inner * q : inner * (q + 1)]

        @pl.when(g == jnp.where(place < 2, 1, 0))
        def _():
            send_strips()

    @pl.when(jnp.logical_and(middle, place > 0))
    def _():
        send_pieces()

    @pl.when(r > 0)
    def _():
        row_copy(0).wait_recv()
        for j in range(2):
            put3(X3, j, HIN[0, j])

    @pl.when(r < NR - 1)
    def _():
        row_copy(1).wait_recv()
        for j in range(2):
            put3(X3, R + 2 + j, HIN[1, j])

    @pl.when(jnp.logical_not(hot))
    def _():
        conv1_pairs((0, R))
        finish([(k, 16, C - 16) for k in (0, R - 2)])

    @pl.when(hot)
    def _():
        conv1_pairs((R * (1 - re),))
        finish([((R - 2) * (1 - re), 16, C - 16)])

    @pl.when(jnp.logical_and(middle, place == 0))
    def _():
        send_pieces()

    @pl.when(r > 0)
    def _():
        sel_copy(0).wait_recv()

    @pl.when(r < NR - 1)
    def _():
        sel_copy(1).wait_recv()

    for k in range(4):
        EXT[k] = jnp.zeros((STRIP, CH), f32)
        EXT[k, 2 : 2 + R, :] = SEL[k].astype(f32)

    @pl.when(r > 0)
    def _():
        for k in range(4):
            EXT[k, 0:2, :] = SIN[0, k].astype(f32)[R - 2 : R]
        for j in range(2):
            first, last = HIN[0, j, 0:16, :].astype(f32), HIN[0, j, C - 16 : C, :].astype(f32)
            for k, v in enumerate((first[0:1], first[1:2], last[14:15], last[15:16])):
                XC[k, j : j + 1, :] = v

    @pl.when(r < NR - 1)
    def _():
        for k in range(4):
            EXT[k, R + 2 : R + 4, :] = SIN[1, k].astype(f32)[0:2]
        for j in range(2):
            first, last = HIN[1, j, 0:16, :].astype(f32), HIN[1, j, C - 16 : C, :].astype(f32)
            for k, v in enumerate((first[0:1], first[1:2], last[14:15], last[15:16])):
                XC[k, R + 2 + j : R + 3 + j, :] = v

    def patch(ref, row, first, lanes, value, at):
        cells = ref[row, first : first + 16, lanes * CH : (lanes + 1) * CH].astype(f32)
        rows = lax.broadcasted_iota(jnp.int32, (16, CH), 0)
        ref[row, first : first + 16, lanes * CH : (lanes + 1) * CH] = jnp.where(
            rows == at, value, cells
        ).astype(bf16)

    def taps(columns):
        return jnp.concatenate([v[a : a + v.shape[0] - 2] for a in range(3) for v in columns], 1)

    def outer_left(l0, l1, x0):
        return taps((jnp.where(el == 1, l1, x0), l0, jnp.where(el == 1, x0, l1)))

    def outer_right(r0, r1, x3):
        return taps((jnp.where(er == 1, r1, x3), r0, jnp.where(er == 1, x3, r1)))

    count = SOUT + 2
    lhs = jnp.concatenate(
        [
            outer_left(EXT[0, 0:count], EXT[1, 0:count], XC[0, 0:count]),
            taps((EXT[0, 0:count], XC[0, 0:count], XC[1, 0:count])),
            taps((XC[2, 0:count], XC[3, 0:count], EXT[2, 0:count])),
            outer_right(EXT[2, 0:count], EXT[3, 0:count], XC[3, 0:count]),
        ],
        0,
    )
    strips = gelu(dot(lhs.astype(bf16), wp1[0 : 3 * K3, 0:CH]) + bias1)
    for k in range(4):
        FS[k] = strips[SOUT * k : SOUT * (k + 1)]

    @pl.loop(0, R + 2)
    def _(k):
        patch(F3, k, 0, 0, FS[0, pl.ds(k, 1), :], 0)
        patch(F3, k, C - 16, 2, FS[3, pl.ds(k, 1), :], 15)
        v = FS[1, pl.ds(k, 1), :]
        patch(F3, k, 0, 1, v, 0)
        patch(F3, k, 0, 0, v, 1)
        v = FS[2, pl.ds(k, 1), :]
        patch(F3, k, C - 16, 1, v, 15)
        patch(F3, k, C - 16, 2, v, 14)

    finish([(k, a, a + 16) for k in range(0, R, 2) for a in (0, C - 16)])

    def corner_cell(face, edge, j, at):
        e = 2 * face + edge
        tile = CTB[at // 2, e // 4].astype(f32)
        rows = lax.broadcasted_iota(jnp.int32, tile.shape, 0)
        return jnp.sum(
            jnp.where(rows == 4 * (e % 4) + 2 * j + at % 2, tile, 0.0), 0, keepdims=True
        )

    @pl.when(hot)
    def _():
        s = re

        @pl.loop(0, NF)
        def _(m):
            chosen_copy(h, m).wait_recv()

        for d in range(2):
            corner_copy(h, d).wait_recv()

        fu, eu = adj[0, s, f], adj[1, s, f]
        flip = flips[s, f]
        rows = lax.broadcasted_iota(jnp.int32, (C, C), 0)
        cols = lax.broadcasted_iota(jnp.int32, (C, C), 1)
        order = jnp.where(cols == jnp.where(flip == 1, C - 1 - rows, rows), 1.0, 0.0).astype(bf16)
        near = HIN[s, 0].astype(f32), HIN[s, 1].astype(f32)
        edge = jnp.where(eu == 1, near[1], near[0]).astype(bf16)
        turned = dot(order, jnp.concatenate([x[(R - 1) * s], edge], 1))
        mine = turned[:, 0:CH]
        put3(X3, 1 + (R + 1) * s, turned[:, CH : 2 * CH].astype(bf16))
        for t, v in enumerate(
            (
                jnp.where(eu == 1, near[0], mine),
                jnp.where(eu == 1, near[1], near[0]),
                jnp.where(eu == 1, mine, near[1]),
            )
        ):
            put3(T3, t, v.astype(bf16))
        none = jnp.zeros((1, CH), f32)
        for e in range(2):
            g, ge = adj[0, 2 + e, fu], adj[1, 2 + e, fu] % 2
            cells = [corner_cell(g, eu, j, 3 * ge) for j in range(2)]
            rim = (
                jnp.where(eu == 1, cells[0], none),
                jnp.where(eu == 1, cells[1], cells[0]),
                jnp.where(eu == 1, none, cells[1]),
            )
            for t in range(3):
                patch(T3, t, (C - 16) * e, 2 * e, rim[t], 15 * e)
            g0, e0 = adj[0, 2 + e, f], adj[1, 2 + e, f] % 2
            g, ge, turn = adj[0, s, g0], adj[1, s, g0], flips[s, g0]
            for depth in range(2):
                at = 3 * e0 if depth == 0 else 1 + e0
                at = jnp.where(turn == 1, 3 - at, at)
                EXT[2 * e + depth, pl.ds(1 + (R + 1) * s, 1), :] = corner_cell(g, ge, ge, at)

        for t in range(2):
            k = 2 + (R - 2) * s + t
            patch(X3, k, 0, 0, EXT[0, pl.ds(k, 1), :], 0)
            patch(X3, k, C - 16, 2, EXT[2, pl.ds(k, 1), :], 15)

        near_rows = pl.ds(1 + (R - 1) * s, 10)
        strip = jnp.concatenate(
            [
                outer_left(EXT[0, near_rows], EXT[1, near_rows], XC[0, near_rows]),
                outer_right(EXT[2, near_rows], EXT[3, near_rows], XC[3, near_rows]),
            ],
            0,
        ).astype(bf16)
        lhs = jnp.concatenate(
            [
                jnp.concatenate([T3[t] for t in range(3)], 1),
                jnp.concatenate([X3[1 + (R - 1) * s + t] for t in range(3)], 1),
                strip,
            ],
            0,
        )
        y = gelu(dot(lhs, wp1[0 : 3 * K3, 0:CH]) + bias1)
        put3(F3, (R + 1) * s, dot(order, y[0:C].astype(bf16)).astype(bf16))
        put3(F3, 1 + (R - 1) * s, y[C : 2 * C].astype(bf16))
        patch(F3, 1 + (R - 1) * s, 0, 0, y[2 * C : 2 * C + 1], 0)
        patch(F3, 1 + (R - 1) * s, C - 16, 2, y[2 * C + 8 : 2 * C + 9], 15)
        finish([((R - 2) * s, 0, C)])

    @pl.when(jnp.logical_not(bottom))
    def _():
        @pl.loop(1, NF)
        def _(o):
            col_copy(o, f).wait_send()

        row_copy(0).wait_send()
        sel_copy(0).wait_send()

    @pl.when(r > 0)
    def _():
        row_copy(1).wait_send()
        sel_copy(1).wait_send()

    @pl.when(hot)
    def _():
        @pl.loop(0, NF)
        def _(m):
            piece_copy(m, h).wait_send()

    @pl.when(bottom)
    def _():
        to_relay().wait_send()

    @pl.when(relay)
    def _():
        @pl.loop(1, NF)
        def _(o):
            relay_copy(o).wait_send()

    @pl.when(middle)
    def _():
        @pl.loop(0, NH)
        def _(m):
            chosen_copy(m, f).wait_send()

            @pl.when(has_corner)
            def _():
                corner_copy(m, side).wait_send()


def per_device(
    state_field, adjacency, edge_flips, conv_first, bias_first, conv_second, bias_second,
    norm_gain, up_weight, up_bias, down_weight, down_bias,
):
    vmem = pl.BlockSpec(memory_space=pltpu.VMEM)
    smem = pl.BlockSpec(memory_space=pltpu.SMEM)
    hbm = pl.BlockSpec(memory_space=pl.ANY)
    dma = pltpu.SemaphoreType.DMA
    return pl.pallas_call(
        kernel,
        out_shape=pltpu.VMEM((1, R, C, CH), bf16),
        in_specs=[smem, smem, hbm, hbm, vmem, hbm, vmem, vmem, hbm, vmem, hbm, vmem],
        out_specs=vmem,
        scratch_shapes=[
            pltpu.VMEM((R, C, CH), bf16),
            pltpu.VMEM((4 * K3, 2 * CH), bf16),
            pltpu.VMEM((4 * K3, 2 * CH), bf16),
            pltpu.VMEM(up_weight.shape, bf16),
            pltpu.VMEM(down_weight.shape, bf16),
            pltpu.VMEM((R + 4, C, K3), bf16),
            pltpu.VMEM((R + 2, C, K3), bf16),
            pltpu.VMEM((3, C, K3), bf16),
            pltpu.VMEM((R - 4, C - 32, CH), bf16),
            pltpu.VMEM((4, R, CH), bf16),
            pltpu.VMEM((NF, 4, R, CH), bf16),
            pltpu.VMEM((2, 2, C, CH), bf16),
            pltpu.VMEM((NH, 2, PIECE, CH), bf16),
            pltpu.VMEM((NH // 4, 16, CH), bf16),
            pltpu.VMEM((2, NH // 4, 16, CH), bf16),
            pltpu.VMEM((NH, 2, PIECE, CH), bf16),
            pltpu.VMEM((4, R, CH), bf16),
            pltpu.VMEM((2, 4, R, CH), bf16),
            pltpu.VMEM((4, STRIP, CH), f32),
            pltpu.VMEM((4, STRIP, CH), f32),
            pltpu.VMEM((4, SOUT, CH), f32),
            dma((7,)), dma((1,)), dma((1,)), dma((NF,)), dma((NF,)), dma((NF,)), dma((2,)), dma((2,)),
            dma((NF,)), dma((NH,)), dma((NH,)), dma((2,)), dma((NH,)), dma((NF,)),
            dma((2,)), dma((2,)),
        ],
        compiler_params=pltpu.CompilerParams(
            collective_id=0, has_side_effects=True, vmem_limit_bytes=56 << 20
        ),
        cost_estimate=pl.CostEstimate(
            flops=3_500_000_000, bytes_accessed=3_000_000, transcendentals=2_600_000
        ),
    )(
        jnp.transpose(adjacency, (0, 2, 1)), jnp.transpose(edge_flips), state_field,
        conv_first.reshape(9 * CH, CH), bias_first.reshape(1, CH),
        conv_second.reshape(9 * CH, CH), bias_second.reshape(1, CH),
        norm_gain.reshape(1, CH), up_weight, up_bias.reshape(1, -1),
        down_weight, down_bias.reshape(1, CH),
    )


def solution(mesh):
    in_specs = (P("face", "row", None, None), P(), P(), P(), P(), P(), P(), P(), P(), P(), P(), P())
    out_specs = P("face", "row", None, None)
    return jax.shard_map(
        per_device, mesh=mesh, in_specs=in_specs, out_specs=out_specs, check_vma=False
    )
```

```python
import jax
import jax.numpy as jnp
from jax import lax
from jax.experimental import pallas as pl
from jax.experimental.pallas import tpu as pltpu
from jax.sharding import PartitionSpec as P

MESH = pl.DeviceIdType.MESH
bf16 = jnp.bfloat16
f32 = jnp.float32

NF = 8
NR = 16
R = 16
C = 256
CH = 128
K3 = 3 * CH
NH = 2 * NF
PIECE = C // NF
STRIP = 32
SOUT = 24


def dot(a, b):
    return jnp.dot(a, b, preferred_element_type=f32)


def gelu(v):
    return (0.5 * v) * (1.0 + lax.erf(v * 0.7071067811865476))


def put3(ref, row, v):
    zero = jnp.zeros((1, CH), bf16)
    ref[row, :, 0:CH] = jnp.concatenate([zero, v[:-1]], 0)
    ref[row, :, CH : 2 * CH] = v
    ref[row, :, 2 * CH : K3] = jnp.concatenate([v[1:], zero], 0)


def kernel(
    adj, flips, x_hbm, w1_hbm, b1, w2_hbm, b2, gain, wu_hbm, bu, wd_hbm, bd,
    out,
    x, wp1, wp2, wu, wd, X3, F3, T3, NS, P15, COL, HIN, PB, CT, CTB, ST, SEL, SIN, EXT, XC, FS,
    locS, viaS, viaR, relS, colS, colR, rowS, rowR, pbS, pbR, ctS, ctR, stS, stR, selS, selR,
):
    f = lax.axis_index("face")
    r = lax.axis_index("row")
    top = r == 0
    bottom = r == NR - 1
    hot = jnp.logical_or(top, bottom)
    middle = r == 1
    relay = r == NR - 2
    re = jnp.where(bottom, 1, 0)
    h = 2 * f + re
    place = f % 4

    def hot_device(m):
        return {"face": m // 2, "row": (m % 2) * (NR - 1)}

    local = [
        pltpu.make_async_copy(src, dst, locS.at[i])
        for i, (src, dst) in enumerate(
            (
                (x_hbm.at[0], x),
                (w1_hbm, wp1.at[pl.ds(0, 3 * K3), pl.ds(0, CH)]),
                (w1_hbm, wp1.at[pl.ds(K3, 3 * K3), pl.ds(CH, CH)]),
                (w2_hbm, wp2.at[pl.ds(0, 3 * K3), pl.ds(0, CH)]),
                (w2_hbm, wp2.at[pl.ds(K3, 3 * K3), pl.ds(CH, CH)]),
                (wu_hbm, wu),
                (wd_hbm, wd),
            )
        )
    ]
    for copy in local:
        copy.start()

    barrier = pltpu.get_barrier_semaphore()

    def greet(device):
        pl.semaphore_signal(barrier, inc=1, device_id=device, device_id_type=MESH)

    @pl.when(middle)
    def _():
        @pl.loop(0, NF)
        def _(o):
            greet({"face": o, "row": NR - 1})

        @pl.loop(0, NF)
        def _(o):
            greet({"face": o, "row": 0})

    @pl.loop(1, NF)
    def _(o):
        greet({"face": (f + o) % NF, "row": jnp.where(bottom, NR - 2, r)})

    @pl.when(r > 0)
    def _():
        greet({"face": f, "row": r - 1})

    @pl.when(r < NR - 1)
    def _():
        greet({"face": f, "row": r + 1})

    def col_copy(o, slot):
        return pltpu.make_async_remote_copy(
            src_ref=COL.at[slot], dst_ref=COL.at[slot],
            send_sem=colS.at[o], recv_sem=colR.at[slot],
            device_id={"face": (f + o) % NF, "row": r}, device_id_type=MESH,
        )

    def row_copy(d):
        return pltpu.make_async_remote_copy(
            src_ref=x_hbm.at[0, pl.ds((1 - d) * (R - 2), 2)], dst_ref=HIN.at[d],
            send_sem=rowS.at[d], recv_sem=rowR.at[d],
            device_id={"face": f, "row": r + 1 - 2 * d}, device_id_type=MESH,
        )

    def piece_copy(m, slot):
        return pltpu.make_async_remote_copy(
            src_ref=x_hbm.at[
                0, pl.ds(re * (R - 2), 2), pl.ds(pl.multiple_of(m * PIECE, PIECE), PIECE)
            ],
            dst_ref=PB.at[slot],
            send_sem=pbS.at[m], recv_sem=pbR.at[slot],
            device_id={"face": m, "row": 1}, device_id_type=MESH,
        )

    def to_relay():
        return pltpu.make_async_remote_copy(
            src_ref=COL.at[f], dst_ref=P15, send_sem=viaS.at[0], recv_sem=viaR.at[0],
            device_id={"face": f, "row": NR - 2}, device_id_type=MESH,
        )

    def relay_copy(o):
        return pltpu.make_async_remote_copy(
            src_ref=P15, dst_ref=COL.at[f], send_sem=relS.at[o], recv_sem=colR.at[f],
            device_id={"face": (f + o) % NF, "row": NR - 1}, device_id_type=MESH,
        )

    def send_end_row():
        @pl.loop(0, NF)
        def _(o):
            piece_copy((f + o) % NF, h).start()

    def send_first():
        busy = jnp.logical_or(top, relay)

        @pl.when(busy)
        def _():
            pl.semaphore_wait(barrier, 2 * NF)

        @pl.when(jnp.logical_not(busy))
        def _():
            pl.semaphore_wait(barrier, NF + 1)

        @pl.loop(1, NF)
        def _(o):
            col_copy(o, f).start()

        @pl.when(top)
        def _():
            send_end_row()

        row_copy(0).start()

        @pl.when(r > 0)
        def _():
            row_copy(1).start()

        @pl.when(relay)
        def _():
            to_relay().wait_recv()

            @pl.loop(1, NF)
            def _(o):
                relay_copy(o).start()

    @pl.when(bottom)
    def _():
        pl.semaphore_wait(barrier, NF + 1)
        send_end_row()
        row_copy(1).start()

    zero = jnp.zeros((K3, CH), bf16)
    for ref in (wp1, wp2):
        ref[3 * K3 : 4 * K3, 0:CH] = zero
        ref[0:K3, CH : 2 * CH] = zero
    bias1 = b1[...]
    bias2 = b2[...]
    norm_gain = gain[...]
    bias_up = bu[...]
    bias_down = bd[...]
    local[0].wait()

    def column(c):
        base = (c // 16) * 16
        rows = [x[i, base : base + 16, :].astype(f32)[c - base : c - base + 1] for i in range(R)]
        return jnp.concatenate(rows, 0)

    for k, c in enumerate((0, 1, C - 2, C - 1)):
        own = column(c)
        COL[f, k] = own.astype(bf16)
        XC[k] = jnp.zeros((STRIP, CH), f32)
        XC[k, 2 : 2 + R, :] = own

    @pl.when(bottom)
    def _():
        to_relay().start()

    def send_at(point):
        @pl.when(jnp.logical_and(jnp.where(place == 3, 0, jnp.where(place == 0, 2, 1)) == point, jnp.logical_not(bottom)))
        def _():
            send_first()

    send_at(0)

    @pl.loop(0, R)
    def _(i):
        put3(X3, i + 2, x[i])

    def conv1_pairs(starts):
        lhs = jnp.concatenate(
            [jnp.concatenate([X3[k + t] for t in range(4)], 1) for k in starts], 0
        )
        y = dot(lhs, wp1[...])
        for q, k in enumerate(starts):
            for j in range(2):
                v = y[C * q : C * (q + 1), CH * j : CH * (j + 1)]
                put3(F3, k + j, gelu(v + bias1).astype(bf16))

    local[1].wait()
    local[2].wait()
    conv1_pairs((2,))
    send_at(1)

    @pl.loop(0, 2)
    def _(g):
        conv1_pairs([4 + 6 * g + 2 * i for i in range(3)])

    send_at(2)

    for copy in local[3:]:
        copy.wait()

    def conv2_norm(segments):
        lhs = jnp.concatenate(
            [jnp.concatenate([F3[k + t, a:b, :] for t in range(4)], 1) for k, a, b in segments], 0
        )
        y = dot(lhs, wp2[...])
        parts, at = [], 0
        for k, a, b in segments:
            parts += [y[at : at + b - a, CH * j : CH * (j + 1)] for j in range(2)]
            at += b - a
        second = jnp.concatenate(parts, 0) + bias2
        second = second - jnp.mean(second, -1, keepdims=True)
        spread = jnp.mean(second * second, -1, keepdims=True)
        return (second * lax.rsqrt(spread + 1e-6) * norm_gain).astype(bf16)

    def pointwise(normed, skip):
        hidden = gelu(dot(normed, wu[...]) + bias_up).astype(bf16)
        return (skip.astype(f32) + (dot(hidden, wd[...]) + bias_down)).astype(bf16)

    def finish(segments):
        cells = [(k + j, a, b) for k, a, b in segments for j in range(2)]
        skip = jnp.concatenate([x[k, a:b, :] for k, a, b in cells], 0)
        mixed, at = pointwise(conv2_norm(segments), skip), 0
        for k, a, b in cells:
            out[0, k, a:b, :] = mixed[at : at + b - a]
            at += b - a

    fl, el = adj[0, 2, f], adj[1, 2, f] % 2
    fr, er = adj[0, 3, f], adj[1, 3, f] % 2

    def sel_copy(d):
        return pltpu.make_async_remote_copy(
            src_ref=SEL, dst_ref=SIN.at[d],
            send_sem=selS.at[d], recv_sem=selR.at[d],
            device_id={"face": f, "row": r + 1 - 2 * d}, device_id_type=MESH,
        )

    def send_strips():
        @pl.loop(1, NF)
        def _(o):
            col_copy(o, (f + NF - o) % NF).wait_recv()

        SEL[0] = COL[fl, 3 * el]
        SEL[1] = COL[fl, 1 + el]
        SEL[2] = COL[fr, 3 * er]
        SEL[3] = COL[fr, 1 + er]

        @pl.when(r < NR - 1)
        def _():
            sel_copy(0).start()

        @pl.when(r > 0)
        def _():
            sel_copy(1).start()

    def chosen_copy(m, slot):
        return pltpu.make_async_remote_copy(
            src_ref=ST.at[m],
            dst_ref=HIN.at[m % 2, pl.ds(0, 2), pl.ds(pl.multiple_of(slot * PIECE, PIECE), PIECE)],
            send_sem=stS.at[m], recv_sem=stR.at[slot],
            device_id=hot_device(m), device_id_type=MESH,
        )

    def corner_copy(m, side):
        return pltpu.make_async_remote_copy(
            src_ref=CT, dst_ref=CTB.at[side],
            send_sem=ctS.at[m], recv_sem=ctR.at[side],
            device_id=hot_device(m), device_id_type=MESH,
        )

    has_corner = jnp.logical_or(f == 0, f == NF - 1)
    side = jnp.where(f == 0, 0, 1)

    def order_of(o):
        return 2 * (o % NF) + o // NF

    def send_pieces():
        @pl.loop(0, NH)
        def _(m):
            pltpu.make_async_remote_copy(
                src_ref=ST.at[m], dst_ref=PB.at[m], send_sem=stS.at[m], recv_sem=pbR.at[m],
                device_id=hot_device(m), device_id_type=MESH,
            ).wait_recv()

        @pl.when(has_corner)
        def _():
            for g in range(NH // 4):
                cells = []
                for e in range(4 * g, 4 * g + 4):
                    for j in range(2):
                        first = PB[e, j, 0:16, :].astype(f32)[0:2]
                        last = PB[e, j, PIECE - 16 : PIECE, :].astype(f32)[14:16]
                        cells.append(jnp.where(f == 0, first, last))
                CT[g] = jnp.concatenate(cells, 0).astype(bf16)

        @pl.loop(0, NH)
        def _(o):
            m = order_of(o)
            ST[m] = PB[2 * adj[0, m % 2, m // 2] + adj[1, m % 2, m // 2]]
            chosen_copy(m, f).start()

            @pl.when(has_corner)
            def _():
                corner_copy(m, side).start()

    inner = C - 32
    half = R // 2 - 2

    @pl.loop(0, 2)
    def _(g):
        normed = conv2_norm([(2 + half * g + 2 * i, 16, C - 16) for i in range(half // 2)])
        for i in range(half):
            NS[half * g + i] = normed[inner * i : inner * (i + 1)]

    send_strips()

    @pl.loop(0, 2)
    def _(g):
        rows = [half * g + i for i in range(half)]
        skip = jnp.concatenate([x[2 + i, 16 : C - 16, :] for i in rows], 0)
        mixed = pointwise(jnp.concatenate([NS[i] for i in rows], 0), skip)
        for q, i in enumerate(rows):
            out[0, 2 + i, 16 : C - 16, :] = mixed[inner * q : inner * (q + 1)]

        @pl.when(jnp.logical_and(middle, jnp.logical_and(place > 0, g == jnp.where(place == 1, 1, 0))))
        def _():
            send_pieces()

    @pl.when(r > 0)
    def _():
        row_copy(0).wait_recv()
        for j in range(2):
            put3(X3, j, HIN[0, j])

    @pl.when(r < NR - 1)
    def _():
        row_copy(1).wait_recv()
        for j in range(2):
            put3(X3, R + 2 + j, HIN[1, j])

    @pl.when(jnp.logical_not(hot))
    def _():
        conv1_pairs((0, R))
        finish([(k, 16, C - 16) for k in (0, R - 2)])

    @pl.when(hot)
    def _():
        conv1_pairs((R * (1 - re),))
        finish([((R - 2) * (1 - re), 16, C - 16)])

    @pl.when(jnp.logical_and(middle, place == 0))
    def _():
        send_pieces()

    @pl.when(r > 0)
    def _():
        sel_copy(0).wait_recv()

    @pl.when(r < NR - 1)
    def _():
        sel_copy(1).wait_recv()

    for k in range(4):
        EXT[k] = jnp.zeros((STRIP, CH), f32)
        EXT[k, 2 : 2 + R, :] = SEL[k].astype(f32)

    @pl.when(r > 0)
    def _():
        for k in range(4):
            EXT[k, 0:2, :] = SIN[0, k].astype(f32)[R - 2 : R]
        for j in range(2):
            first, last = HIN[0, j, 0:16, :].astype(f32), HIN[0, j, C - 16 : C, :].astype(f32)
            for k, v in enumerate((first[0:1], first[1:2], last[14:15], last[15:16])):
                XC[k, j : j + 1, :] = v

    @pl.when(r < NR - 1)
    def _():
        for k in range(4):
            EXT[k, R + 2 : R + 4, :] = SIN[1, k].astype(f32)[0:2]
        for j in range(2):
            first, last = HIN[1, j, 0:16, :].astype(f32), HIN[1, j, C - 16 : C, :].astype(f32)
            for k, v in enumerate((first[0:1], first[1:2], last[14:15], last[15:16])):
                XC[k, R + 2 + j : R + 3 + j, :] = v

    def patch(ref, row, first, lanes, value, at):
        cells = ref[row, first : first + 16, lanes * CH : (lanes + 1) * CH].astype(f32)
        rows = lax.broadcasted_iota(jnp.int32, (16, CH), 0)
        ref[row, first : first + 16, lanes * CH : (lanes + 1) * CH] = jnp.where(
            rows == at, value, cells
        ).astype(bf16)

    def taps(columns):
        return jnp.concatenate([v[a : a + v.shape[0] - 2] for a in range(3) for v in columns], 1)

    def outer_left(l0, l1, x0):
        return taps((jnp.where(el == 1, l1, x0), l0, jnp.where(el == 1, x0, l1)))

    def outer_right(r0, r1, x3):
        return taps((jnp.where(er == 1, r1, x3), r0, jnp.where(er == 1, x3, r1)))

    count = SOUT + 2
    lhs = jnp.concatenate(
        [
            outer_left(EXT[0, 0:count], EXT[1, 0:count], XC[0, 0:count]),
            taps((EXT[0, 0:count], XC[0, 0:count], XC[1, 0:count])),
            taps((XC[2, 0:count], XC[3, 0:count], EXT[2, 0:count])),
            outer_right(EXT[2, 0:count], EXT[3, 0:count], XC[3, 0:count]),
        ],
        0,
    )
    strips = gelu(dot(lhs.astype(bf16), wp1[0 : 3 * K3, 0:CH]) + bias1)
    for k in range(4):
        FS[k] = strips[SOUT * k : SOUT * (k + 1)]

    @pl.loop(0, R + 2)
    def _(k):
        patch(F3, k, 0, 0, FS[0, pl.ds(k, 1), :], 0)
        patch(F3, k, C - 16, 2, FS[3, pl.ds(k, 1), :], 15)
        v = FS[1, pl.ds(k, 1), :]
        patch(F3, k, 0, 1, v, 0)
        patch(F3, k, 0, 0, v, 1)
        v = FS[2, pl.ds(k, 1), :]
        patch(F3, k, C - 16, 1, v, 15)
        patch(F3, k, C - 16, 2, v, 14)

    finish([(k, a, a + 16) for k in range(0, R, 2) for a in (0, C - 16)])

    def corner_cell(face, edge, j, at):
        e = 2 * face + edge
        tile = CTB[at // 2, e // 4].astype(f32)
        rows = lax.broadcasted_iota(jnp.int32, tile.shape, 0)
        return jnp.sum(
            jnp.where(rows == 4 * (e % 4) + 2 * j + at % 2, tile, 0.0), 0, keepdims=True
        )

    @pl.when(hot)
    def _():
        s = re

        @pl.loop(0, NF)
        def _(m):
            chosen_copy(h, m).wait_recv()

        for d in range(2):
            corner_copy(h, d).wait_recv()

        fu, eu = adj[0, s, f], adj[1, s, f]
        flip = flips[s, f]
        rows = lax.broadcasted_iota(jnp.int32, (C, C), 0)
        cols = lax.broadcasted_iota(jnp.int32, (C, C), 1)
        order = jnp.where(cols == jnp.where(flip == 1, C - 1 - rows, rows), 1.0, 0.0).astype(bf16)
        near = HIN[s, 0].astype(f32), HIN[s, 1].astype(f32)
        edge = jnp.where(eu == 1, near[1], near[0]).astype(bf16)
        turned = dot(order, jnp.concatenate([x[(R - 1) * s], edge], 1))
        mine = turned[:, 0:CH]
        put3(X3, 1 + (R + 1) * s, turned[:, CH : 2 * CH].astype(bf16))
        for t, v in enumerate(
            (
                jnp.where(eu == 1, near[0], mine),
                jnp.where(eu == 1, near[1], near[0]),
                jnp.where(eu == 1, mine, near[1]),
            )
        ):
            put3(T3, t, v.astype(bf16))
        none = jnp.zeros((1, CH), f32)
        for e in range(2):
            g, ge = adj[0, 2 + e, fu], adj[1, 2 + e, fu] % 2
            cells = [corner_cell(g, eu, j, 3 * ge) for j in range(2)]
            rim = (
                jnp.where(eu == 1, cells[0], none),
                jnp.where(eu == 1, cells[1], cells[0]),
                jnp.where(eu == 1, none, cells[1]),
            )
            for t in range(3):
                patch(T3, t, (C - 16) * e, 2 * e, rim[t], 15 * e)
            g0, e0 = adj[0, 2 + e, f], adj[1, 2 + e, f] % 2
            g, ge, turn = adj[0, s, g0], adj[1, s, g0], flips[s, g0]
            for depth in range(2):
                at = 3 * e0 if depth == 0 else 1 + e0
                at = jnp.where(turn == 1, 3 - at, at)
                EXT[2 * e + depth, pl.ds(1 + (R + 1) * s, 1), :] = corner_cell(g, ge, ge, at)

        for t in range(2):
            k = 2 + (R - 2) * s + t
            patch(X3, k, 0, 0, EXT[0, pl.ds(k, 1), :], 0)
            patch(X3, k, C - 16, 2, EXT[2, pl.ds(k, 1), :], 15)

        near_rows = pl.ds(1 + (R - 1) * s, 10)
        strip = jnp.concatenate(
            [
                outer_left(EXT[0, near_rows], EXT[1, near_rows], XC[0, near_rows]),
                outer_right(EXT[2, near_rows], EXT[3, near_rows], XC[3, near_rows]),
            ],
            0,
        ).astype(bf16)
        lhs = jnp.concatenate(
            [
                jnp.concatenate([T3[t] for t in range(3)], 1),
                jnp.concatenate([X3[1 + (R - 1) * s + t] for t in range(3)], 1),
                strip,
            ],
            0,
        )
        y = gelu(dot(lhs, wp1[0 : 3 * K3, 0:CH]) + bias1)
        put3(F3, (R + 1) * s, dot(order, y[0:C].astype(bf16)).astype(bf16))
        put3(F3, 1 + (R - 1) * s, y[C : 2 * C].astype(bf16))
        patch(F3, 1 + (R - 1) * s, 0, 0, y[2 * C : 2 * C + 1], 0)
        patch(F3, 1 + (R - 1) * s, C - 16, 2, y[2 * C + 8 : 2 * C + 9], 15)
        finish([((R - 2) * s, 0, C)])

    @pl.when(jnp.logical_not(bottom))
    def _():
        @pl.loop(1, NF)
        def _(o):
            col_copy(o, f).wait_send()

        row_copy(0).wait_send()
        sel_copy(0).wait_send()

    @pl.when(r > 0)
    def _():
        row_copy(1).wait_send()
        sel_copy(1).wait_send()

    @pl.when(hot)
    def _():
        @pl.loop(0, NF)
        def _(m):
            piece_copy(m, h).wait_send()

    @pl.when(bottom)
    def _():
        to_relay().wait_send()

    @pl.when(relay)
    def _():
        @pl.loop(1, NF)
        def _(o):
            relay_copy(o).wait_send()

    @pl.when(middle)
    def _():
        @pl.loop(0, NH)
        def _(m):
            chosen_copy(m, f).wait_send()

            @pl.when(has_corner)
            def _():
                corner_copy(m, side).wait_send()


def per_device(
    state_field, adjacency, edge_flips, conv_first, bias_first, conv_second, bias_second,
    norm_gain, up_weight, up_bias, down_weight, down_bias,
):
    vmem = pl.BlockSpec(memory_space=pltpu.VMEM)
    smem = pl.BlockSpec(memory_space=pltpu.SMEM)
    hbm = pl.BlockSpec(memory_space=pl.ANY)
    dma = pltpu.SemaphoreType.DMA
    return pl.pallas_call(
        kernel,
        out_shape=pltpu.VMEM((1, R, C, CH), bf16),
        in_specs=[smem, smem, hbm, hbm, vmem, hbm, vmem, vmem, hbm, vmem, hbm, vmem],
        out_specs=vmem,
        scratch_shapes=[
            pltpu.VMEM((R, C, CH), bf16),
            pltpu.VMEM((4 * K3, 2 * CH), bf16),
            pltpu.VMEM((4 * K3, 2 * CH), bf16),
            pltpu.VMEM(up_weight.shape, bf16),
            pltpu.VMEM(down_weight.shape, bf16),
            pltpu.VMEM((R + 4, C, K3), bf16),
            pltpu.VMEM((R + 2, C, K3), bf16),
            pltpu.VMEM((3, C, K3), bf16),
            pltpu.VMEM((R - 4, C - 32, CH), bf16),
            pltpu.VMEM((4, R, CH), bf16),
            pltpu.VMEM((NF, 4, R, CH), bf16),
            pltpu.VMEM((2, 2, C, CH), bf16),
            pltpu.VMEM((NH, 2, PIECE, CH), bf16),
            pltpu.VMEM((NH // 4, 16, CH), bf16),
            pltpu.VMEM((2, NH // 4, 16, CH), bf16),
            pltpu.VMEM((NH, 2, PIECE, CH), bf16),
            pltpu.VMEM((4, R, CH), bf16),
            pltpu.VMEM((2, 4, R, CH), bf16),
            pltpu.VMEM((4, STRIP, CH), f32),
            pltpu.VMEM((4, STRIP, CH), f32),
            pltpu.VMEM((4, SOUT, CH), f32),
            dma((7,)), dma((1,)), dma((1,)), dma((NF,)), dma((NF,)), dma((NF,)), dma((2,)), dma((2,)),
            dma((NF,)), dma((NH,)), dma((NH,)), dma((2,)), dma((NH,)), dma((NF,)),
            dma((2,)), dma((2,)),
        ],
        compiler_params=pltpu.CompilerParams(
            collective_id=0, has_side_effects=True, vmem_limit_bytes=56 << 20
        ),
        cost_estimate=pl.CostEstimate(
            flops=3_500_000_000, bytes_accessed=3_000_000, transcendentals=2_600_000
        ),
    )(
        jnp.transpose(adjacency, (0, 2, 1)), jnp.transpose(edge_flips), state_field,
        conv_first.reshape(9 * CH, CH), bias_first.reshape(1, CH),
        conv_second.reshape(9 * CH, CH), bias_second.reshape(1, CH),
        norm_gain.reshape(1, CH), up_weight, up_bias.reshape(1, -1),
        down_weight, down_bias.reshape(1, CH),
    )


def solution(mesh):
    in_specs = (P("face", "row", None, None), P(), P(), P(), P(), P(), P(), P(), P(), P(), P(), P())
    out_specs = P("face", "row", None, None)
    return jax.shard_map(
        per_device, mesh=mesh, in_specs=in_specs, out_specs=out_specs, check_vma=False
    )
```

```python
import jax
import jax.numpy as jnp
from jax import lax
from jax.experimental import pallas as pl
from jax.experimental.pallas import tpu as pltpu
from jax.sharding import PartitionSpec as P

MESH = pl.DeviceIdType.MESH
bf16 = jnp.bfloat16
f32 = jnp.float32

NF = 8
NR = 16
R = 16
C = 256
CH = 128
K3 = 3 * CH
NH = 2 * NF
PIECE = C // NF
STRIP = 32
SOUT = 24


def dot(a, b):
    return jnp.dot(a, b, preferred_element_type=f32)


def gelu(v):
    return (0.5 * v) * (1.0 + lax.erf(v * 0.7071067811865476))


def put3(ref, row, v):
    zero = jnp.zeros((1, CH), bf16)
    ref[row, :, 0:CH] = jnp.concatenate([zero, v[:-1]], 0)
    ref[row, :, CH : 2 * CH] = v
    ref[row, :, 2 * CH : K3] = jnp.concatenate([v[1:], zero], 0)


def kernel(
    adj, flips, x_hbm, w1_hbm, b1, w2_hbm, b2, gain, wu_hbm, bu, wd_hbm, bd,
    out,
    x, wp1, wp2, wu, wd, X3, F3, T3, NS, P15, COL, HIN, PB, CT, CTB, ST, SEL, SIN, EXT, XC, FS,
    locS, viaS, viaR, relS, colS, colR, rowS, rowR, pbS, pbR, ctS, ctR, stS, stR, selS, selR,
):
    f = lax.axis_index("face")
    r = lax.axis_index("row")
    top = r == 0
    bottom = r == NR - 1
    hot = jnp.logical_or(top, bottom)
    middle = r == 1
    here = (f + 3) % NF
    relay = r == NR - 2
    re = jnp.where(bottom, 1, 0)
    h = 2 * f + re
    place = f % 4

    def hot_device(m):
        return {"face": m // 2, "row": (m % 2) * (NR - 1)}

    local = [
        pltpu.make_async_copy(src, dst, locS.at[i])
        for i, (src, dst) in enumerate(
            (
                (x_hbm.at[0], x),
                (w1_hbm, wp1.at[pl.ds(0, 3 * K3), pl.ds(0, CH)]),
                (w1_hbm, wp1.at[pl.ds(K3, 3 * K3), pl.ds(CH, CH)]),
                (w2_hbm, wp2.at[pl.ds(0, 3 * K3), pl.ds(0, CH)]),
                (w2_hbm, wp2.at[pl.ds(K3, 3 * K3), pl.ds(CH, CH)]),
                (wu_hbm, wu),
                (wd_hbm, wd),
            )
        )
    ]
    for copy in local:
        copy.start()

    barrier = pltpu.get_barrier_semaphore()

    def greet(device):
        pl.semaphore_signal(barrier, inc=1, device_id=device, device_id_type=MESH)

    @pl.when(middle)
    def _():
        @pl.loop(0, NF)
        def _(o):
            greet({"face": o, "row": NR - 1})

        @pl.loop(0, NF)
        def _(o):
            greet({"face": o, "row": 0})

    @pl.loop(1, NF)
    def _(o):
        greet({"face": (f + o) % NF, "row": jnp.where(bottom, NR - 2, r)})

    @pl.when(r > 0)
    def _():
        greet({"face": f, "row": r - 1})

    @pl.when(r < NR - 1)
    def _():
        greet({"face": f, "row": r + 1})

    def col_copy(o, slot):
        return pltpu.make_async_remote_copy(
            src_ref=COL.at[slot], dst_ref=COL.at[slot],
            send_sem=colS.at[o], recv_sem=colR.at[slot],
            device_id={"face": (f + o) % NF, "row": r}, device_id_type=MESH,
        )

    def row_copy(d):
        return pltpu.make_async_remote_copy(
            src_ref=x_hbm.at[0, pl.ds((1 - d) * (R - 2), 2)], dst_ref=HIN.at[d],
            send_sem=rowS.at[d], recv_sem=rowR.at[d],
            device_id={"face": f, "row": r + 1 - 2 * d}, device_id_type=MESH,
        )

    def piece_copy(m, slot):
        return pltpu.make_async_remote_copy(
            src_ref=x_hbm.at[
                0, pl.ds(re * (R - 2), 2), pl.ds(pl.multiple_of(m * PIECE, PIECE), PIECE)
            ],
            dst_ref=PB.at[slot],
            send_sem=pbS.at[m], recv_sem=pbR.at[slot],
            device_id={"face": (m + NF - 3) % NF, "row": 1}, device_id_type=MESH,
        )

    def to_relay():
        return pltpu.make_async_remote_copy(
            src_ref=COL.at[f], dst_ref=P15, send_sem=viaS.at[0], recv_sem=viaR.at[0],
            device_id={"face": f, "row": NR - 2}, device_id_type=MESH,
        )

    def relay_copy(o):
        return pltpu.make_async_remote_copy(
            src_ref=P15, dst_ref=COL.at[f], send_sem=relS.at[o], recv_sem=colR.at[f],
            device_id={"face": (f + o) % NF, "row": NR - 1}, device_id_type=MESH,
        )

    def send_end_row():
        @pl.loop(0, NF)
        def _(o):
            piece_copy((f + o) % NF, h).start()

    def send_first():
        busy = jnp.logical_or(top, relay)

        @pl.when(busy)
        def _():
            pl.semaphore_wait(barrier, 2 * NF)

        @pl.when(jnp.logical_not(busy))
        def _():
            pl.semaphore_wait(barrier, NF + 1)

        @pl.loop(1, NF)
        def _(o):
            col_copy(o, f).start()

        @pl.when(top)
        def _():
            send_end_row()

        row_copy(0).start()

        @pl.when(r > 0)
        def _():
            row_copy(1).start()

        @pl.when(relay)
        def _():
            to_relay().wait_recv()

            @pl.loop(1, NF)
            def _(o):
                relay_copy(o).start()

    @pl.when(bottom)
    def _():
        pl.semaphore_wait(barrier, NF + 1)
        send_end_row()
        row_copy(1).start()

    zero = jnp.zeros((K3, CH), bf16)
    for ref in (wp1, wp2):
        ref[3 * K3 : 4 * K3, 0:CH] = zero
        ref[0:K3, CH : 2 * CH] = zero
    bias1 = b1[...]
    bias2 = b2[...]
    norm_gain = gain[...]
    bias_up = bu[...]
    bias_down = bd[...]
    local[0].wait()

    def column(c):
        base = (c // 16) * 16
        rows = [x[i, base : base + 16, :].astype(f32)[c - base : c - base + 1] for i in range(R)]
        return jnp.concatenate(rows, 0)

    for k, c in enumerate((0, 1, C - 2, C - 1)):
        own = column(c)
        COL[f, k] = own.astype(bf16)
        XC[k] = jnp.zeros((STRIP, CH), f32)
        XC[k, 2 : 2 + R, :] = own

    @pl.when(bottom)
    def _():
        to_relay().start()

    def send_at(point):
        @pl.when(jnp.logical_and(jnp.where(place == 3, 0, jnp.where(place == 0, 2, 1)) == point, jnp.logical_not(bottom)))
        def _():
            send_first()

    send_at(0)

    @pl.loop(0, R)
    def _(i):
        put3(X3, i + 2, x[i])

    def conv1_pairs(starts):
        lhs = jnp.concatenate(
            [jnp.concatenate([X3[k + t] for t in range(4)], 1) for k in starts], 0
        )
        y = dot(lhs, wp1[...])
        for q, k in enumerate(starts):
            for j in range(2):
                v = y[C * q : C * (q + 1), CH * j : CH * (j + 1)]
                put3(F3, k + j, gelu(v + bias1).astype(bf16))

    local[1].wait()
    local[2].wait()
    conv1_pairs((2,))
    send_at(1)

    @pl.loop(0, 2)
    def _(g):
        conv1_pairs([4 + 6 * g + 2 * i for i in range(3)])

    send_at(2)

    for copy in local[3:]:
        copy.wait()

    def conv2_norm(segments):
        lhs = jnp.concatenate(
            [jnp.concatenate([F3[k + t, a:b, :] for t in range(4)], 1) for k, a, b in segments], 0
        )
        y = dot(lhs, wp2[...])
        parts, at = [], 0
        for k, a, b in segments:
            parts += [y[at : at + b - a, CH * j : CH * (j + 1)] for j in range(2)]
            at += b - a
        second = jnp.concatenate(parts, 0) + bias2
        second = second - jnp.mean(second, -1, keepdims=True)
        spread = jnp.mean(second * second, -1, keepdims=True)
        return (second * lax.rsqrt(spread + 1e-6) * norm_gain).astype(bf16)

    def pointwise(normed, skip):
        hidden = gelu(dot(normed, wu[...]) + bias_up).astype(bf16)
        return (skip.astype(f32) + (dot(hidden, wd[...]) + bias_down)).astype(bf16)

    def finish(segments):
        cells = [(k + j, a, b) for k, a, b in segments for j in range(2)]
        skip = jnp.concatenate([x[k, a:b, :] for k, a, b in cells], 0)
        mixed, at = pointwise(conv2_norm(segments), skip), 0
        for k, a, b in cells:
            out[0, k, a:b, :] = mixed[at : at + b - a]
            at += b - a

    fl, el = adj[0, 2, f], adj[1, 2, f] % 2
    fr, er = adj[0, 3, f], adj[1, 3, f] % 2

    def sel_copy(d):
        return pltpu.make_async_remote_copy(
            src_ref=SEL, dst_ref=SIN.at[d],
            send_sem=selS.at[d], recv_sem=selR.at[d],
            device_id={"face": f, "row": r + 1 - 2 * d}, device_id_type=MESH,
        )

    def send_strips():
        @pl.loop(1, NF)
        def _(o):
            col_copy(o, (f + NF - o) % NF).wait_recv()

        SEL[0] = COL[fl, 3 * el]
        SEL[1] = COL[fl, 1 + el]
        SEL[2] = COL[fr, 3 * er]
        SEL[3] = COL[fr, 1 + er]

        @pl.when(r < NR - 1)
        def _():
            sel_copy(0).start()

        @pl.when(r > 0)
        def _():
            sel_copy(1).start()

    def chosen_copy(m, slot):
        return pltpu.make_async_remote_copy(
            src_ref=ST.at[m],
            dst_ref=HIN.at[m % 2, pl.ds(0, 2), pl.ds(pl.multiple_of(slot * PIECE, PIECE), PIECE)],
            send_sem=stS.at[m], recv_sem=stR.at[slot],
            device_id=hot_device(m), device_id_type=MESH,
        )

    def corner_copy(m, side):
        return pltpu.make_async_remote_copy(
            src_ref=CT, dst_ref=CTB.at[side],
            send_sem=ctS.at[m], recv_sem=ctR.at[side],
            device_id=hot_device(m), device_id_type=MESH,
        )

    has_corner = jnp.logical_or(here == 0, here == NF - 1)
    side = jnp.where(here == 0, 0, 1)

    def order_of(o):
        return 2 * (o % NF) + o // NF

    def send_pieces():
        @pl.loop(0, NH)
        def _(m):
            pltpu.make_async_remote_copy(
                src_ref=ST.at[m], dst_ref=PB.at[m], send_sem=stS.at[m], recv_sem=pbR.at[m],
                device_id=hot_device(m), device_id_type=MESH,
            ).wait_recv()

        @pl.when(has_corner)
        def _():
            for g in range(NH // 4):
                cells = []
                for e in range(4 * g, 4 * g + 4):
                    for j in range(2):
                        first = PB[e, j, 0:16, :].astype(f32)[0:2]
                        last = PB[e, j, PIECE - 16 : PIECE, :].astype(f32)[14:16]
                        cells.append(jnp.where(side == 0, first, last))
                CT[g] = jnp.concatenate(cells, 0).astype(bf16)

        @pl.loop(0, NH)
        def _(o):
            m = order_of(o)
            ST[m] = PB[2 * adj[0, m % 2, m // 2] + adj[1, m % 2, m // 2]]
            chosen_copy(m, here).start()

            @pl.when(has_corner)
            def _():
                corner_copy(m, side).start()

    inner = C - 32
    half = R // 2 - 2

    @pl.loop(0, 2)
    def _(g):
        normed = conv2_norm([(2 + half * g + 2 * i, 16, C - 16) for i in range(half // 2)])
        for i in range(half):
            NS[half * g + i] = normed[inner * i : inner * (i + 1)]

    send_strips()

    @pl.loop(0, 2)
    def _(g):
        rows = [half * g + i for i in range(half)]
        skip = jnp.concatenate([x[2 + i, 16 : C - 16, :] for i in rows], 0)
        mixed = pointwise(jnp.concatenate([NS[i] for i in rows], 0), skip)
        for q, i in enumerate(rows):
            out[0, 2 + i, 16 : C - 16, :] = mixed[inner * q : inner * (q + 1)]

        @pl.when(jnp.logical_and(middle, jnp.logical_and(f > 0, g == jnp.where(place < 2, 1, 0))))
        def _():
            send_pieces()

    @pl.when(r > 0)
    def _():
        row_copy(0).wait_recv()
        for j in range(2):
            put3(X3, j, HIN[0, j])

    @pl.when(r < NR - 1)
    def _():
        row_copy(1).wait_recv()
        for j in range(2):
            put3(X3, R + 2 + j, HIN[1, j])

    @pl.when(jnp.logical_not(hot))
    def _():
        conv1_pairs((0, R))
        finish([(k, 16, C - 16) for k in (0, R - 2)])

    @pl.when(hot)
    def _():
        conv1_pairs((R * (1 - re),))

    @pl.when(jnp.logical_and(middle, f == 0))
    def _():
        send_pieces()

    @pl.when(r > 0)
    def _():
        sel_copy(0).wait_recv()

    @pl.when(r < NR - 1)
    def _():
        sel_copy(1).wait_recv()

    for k in range(4):
        EXT[k] = jnp.zeros((STRIP, CH), f32)
        EXT[k, 2 : 2 + R, :] = SEL[k].astype(f32)

    @pl.when(r > 0)
    def _():
        for k in range(4):
            EXT[k, 0:2, :] = SIN[0, k].astype(f32)[R - 2 : R]
        for j in range(2):
            first, last = HIN[0, j, 0:16, :].astype(f32), HIN[0, j, C - 16 : C, :].astype(f32)
            for k, v in enumerate((first[0:1], first[1:2], last[14:15], last[15:16])):
                XC[k, j : j + 1, :] = v

    @pl.when(r < NR - 1)
    def _():
        for k in range(4):
            EXT[k, R + 2 : R + 4, :] = SIN[1, k].astype(f32)[0:2]
        for j in range(2):
            first, last = HIN[1, j, 0:16, :].astype(f32), HIN[1, j, C - 16 : C, :].astype(f32)
            for k, v in enumerate((first[0:1], first[1:2], last[14:15], last[15:16])):
                XC[k, R + 2 + j : R + 3 + j, :] = v

    def patch(ref, row, first, lanes, value, at):
        cells = ref[row, first : first + 16, lanes * CH : (lanes + 1) * CH].astype(f32)
        rows = lax.broadcasted_iota(jnp.int32, (16, CH), 0)
        ref[row, first : first + 16, lanes * CH : (lanes + 1) * CH] = jnp.where(
            rows == at, value, cells
        ).astype(bf16)

    def taps(columns):
        return jnp.concatenate([v[a : a + v.shape[0] - 2] for a in range(3) for v in columns], 1)

    def outer_left(l0, l1, x0):
        return taps((jnp.where(el == 1, l1, x0), l0, jnp.where(el == 1, x0, l1)))

    def outer_right(r0, r1, x3):
        return taps((jnp.where(er == 1, r1, x3), r0, jnp.where(er == 1, x3, r1)))

    count = SOUT + 2
    lhs = jnp.concatenate(
        [
            outer_left(EXT[0, 0:count], EXT[1, 0:count], XC[0, 0:count]),
            taps((EXT[0, 0:count], XC[0, 0:count], XC[1, 0:count])),
            taps((XC[2, 0:count], XC[3, 0:count], EXT[2, 0:count])),
            outer_right(EXT[2, 0:count], EXT[3, 0:count], XC[3, 0:count]),
        ],
        0,
    )
    strips = gelu(dot(lhs.astype(bf16), wp1[0 : 3 * K3, 0:CH]) + bias1)
    for k in range(4):
        FS[k] = strips[SOUT * k : SOUT * (k + 1)]

    edge_row = lax.broadcasted_iota(jnp.int32, (16, 2 * CH), 0)
    first_half = lax.broadcasted_iota(jnp.int32, (16, 2 * CH), 1) < CH

    @pl.loop(0, R + 2)
    def _(k):
        v = [FS[i, pl.ds(k, 1), :] for i in range(4)]
        cells = F3[k, 0:16, 0 : 2 * CH].astype(f32)
        cells = jnp.where(edge_row == 0, jnp.concatenate([v[0], v[1]], 1), cells)
        beside = jnp.logical_and(edge_row == 1, first_half)
        cells = jnp.where(beside, jnp.concatenate([v[1], v[1]], 1), cells)
        F3[k, 0:16, 0 : 2 * CH] = cells.astype(bf16)
        cells = F3[k, C - 16 : C, CH:K3].astype(f32)
        cells = jnp.where(edge_row == 15, jnp.concatenate([v[2], v[3]], 1), cells)
        beside = jnp.logical_and(edge_row == 14, jnp.logical_not(first_half))
        cells = jnp.where(beside, jnp.concatenate([v[2], v[2]], 1), cells)
        F3[k, C - 16 : C, CH:K3] = cells.astype(bf16)

    @pl.when(jnp.logical_not(hot))
    def _():
        finish([(k, a, a + 16) for k in range(0, R, 2) for a in (0, C - 16)])

    @pl.when(hot)
    def _():
        outer = [(k, a, a + 16) for k in range(2, R - 2, 2) for a in (0, C - 16)]
        finish([((R - 2) * (1 - re), 0, C)] + outer)

    def corner_cell(face, edge, j, at):
        e = 2 * face + edge
        tile = CTB[at // 2, e // 4].astype(f32)
        rows = lax.broadcasted_iota(jnp.int32, tile.shape, 0)
        return jnp.sum(
            jnp.where(rows == 4 * (e % 4) + 2 * j + at % 2, tile, 0.0), 0, keepdims=True
        )

    @pl.when(hot)
    def _():
        s = re

        @pl.loop(0, NF)
        def _(m):
            chosen_copy(h, m).wait_recv()

        for d in range(2):
            corner_copy(h, d).wait_recv()

        fu, eu = adj[0, s, f], adj[1, s, f]
        flip = flips[s, f]
        rows = lax.broadcasted_iota(jnp.int32, (C, C), 0)
        cols = lax.broadcasted_iota(jnp.int32, (C, C), 1)
        order = jnp.where(cols == jnp.where(flip == 1, C - 1 - rows, rows), 1.0, 0.0).astype(bf16)
        near = HIN[s, 0].astype(f32), HIN[s, 1].astype(f32)
        edge = jnp.where(eu == 1, near[1], near[0]).astype(bf16)
        turned = dot(order, jnp.concatenate([x[(R - 1) * s], edge], 1))
        mine = turned[:, 0:CH]
        put3(X3, 1 + (R + 1) * s, turned[:, CH : 2 * CH].astype(bf16))
        for t, v in enumerate(
            (
                jnp.where(eu == 1, near[0], mine),
                jnp.where(eu == 1, near[1], near[0]),
                jnp.where(eu == 1, mine, near[1]),
            )
        ):
            put3(T3, t, v.astype(bf16))
        none = jnp.zeros((1, CH), f32)
        for e in range(2):
            g, ge = adj[0, 2 + e, fu], adj[1, 2 + e, fu] % 2
            cells = [corner_cell(g, eu, j, 3 * ge) for j in range(2)]
            rim = (
                jnp.where(eu == 1, cells[0], none),
                jnp.where(eu == 1, cells[1], cells[0]),
                jnp.where(eu == 1, none, cells[1]),
            )
            for t in range(3):
                patch(T3, t, (C - 16) * e, 2 * e, rim[t], 15 * e)
            g0, e0 = adj[0, 2 + e, f], adj[1, 2 + e, f] % 2
            g, ge, turn = adj[0, s, g0], adj[1, s, g0], flips[s, g0]
            for depth in range(2):
                at = 3 * e0 if depth == 0 else 1 + e0
                at = jnp.where(turn == 1, 3 - at, at)
                EXT[2 * e + depth, pl.ds(1 + (R + 1) * s, 1), :] = corner_cell(g, ge, ge, at)

        for t in range(2):
            k = 2 + (R - 2) * s + t
            patch(X3, k, 0, 0, EXT[0, pl.ds(k, 1), :], 0)
            patch(X3, k, C - 16, 2, EXT[2, pl.ds(k, 1), :], 15)

        near_rows = pl.ds(1 + (R - 1) * s, 10)
        strip = jnp.concatenate(
            [
                outer_left(EXT[0, near_rows], EXT[1, near_rows], XC[0, near_rows]),
                outer_right(EXT[2, near_rows], EXT[3, near_rows], XC[3, near_rows]),
            ],
            0,
        ).astype(bf16)
        lhs = jnp.concatenate(
            [
                jnp.concatenate([T3[t] for t in range(3)], 1),
                jnp.concatenate([X3[1 + (R - 1) * s + t] for t in range(3)], 1),
                strip,
            ],
            0,
        )
        y = gelu(dot(lhs, wp1[0 : 3 * K3, 0:CH]) + bias1)
        put3(F3, (R + 1) * s, dot(order, y[0:C].astype(bf16)).astype(bf16))
        put3(F3, 1 + (R - 1) * s, y[C : 2 * C].astype(bf16))
        patch(F3, 1 + (R - 1) * s, 0, 0, y[2 * C : 2 * C + 1], 0)
        patch(F3, 1 + (R - 1) * s, C - 16, 2, y[2 * C + 8 : 2 * C + 9], 15)
        finish([((R - 2) * s, 0, C)])

    @pl.when(jnp.logical_not(bottom))
    def _():
        @pl.loop(1, NF)
        def _(o):
            col_copy(o, f).wait_send()

        row_copy(0).wait_send()
        sel_copy(0).wait_send()

    @pl.when(r > 0)
    def _():
        row_copy(1).wait_send()
        sel_copy(1).wait_send()

    @pl.when(hot)
    def _():
        @pl.loop(0, NF)
        def _(m):
            piece_copy(m, h).wait_send()

    @pl.when(bottom)
    def _():
        to_relay().wait_send()

    @pl.when(relay)
    def _():
        @pl.loop(1, NF)
        def _(o):
            relay_copy(o).wait_send()

    @pl.when(middle)
    def _():
        @pl.loop(0, NH)
        def _(m):
            chosen_copy(m, here).wait_send()

            @pl.when(has_corner)
            def _():
                corner_copy(m, side).wait_send()


def per_device(
    state_field, adjacency, edge_flips, conv_first, bias_first, conv_second, bias_second,
    norm_gain, up_weight, up_bias, down_weight, down_bias,
):
    vmem = pl.BlockSpec(memory_space=pltpu.VMEM)
    smem = pl.BlockSpec(memory_space=pltpu.SMEM)
    hbm = pl.BlockSpec(memory_space=pl.ANY)
    dma = pltpu.SemaphoreType.DMA
    return pl.pallas_call(
        kernel,
        out_shape=pltpu.VMEM((1, R, C, CH), bf16),
        in_specs=[smem, smem, hbm, hbm, vmem, hbm, vmem, vmem, hbm, vmem, hbm, vmem],
        out_specs=vmem,
        scratch_shapes=[
            pltpu.VMEM((R, C, CH), bf16),
            pltpu.VMEM((4 * K3, 2 * CH), bf16),
            pltpu.VMEM((4 * K3, 2 * CH), bf16),
            pltpu.VMEM(up_weight.shape, bf16),
            pltpu.VMEM(down_weight.shape, bf16),
            pltpu.VMEM((R + 4, C, K3), bf16),
            pltpu.VMEM((R + 2, C, K3), bf16),
            pltpu.VMEM((3, C, K3), bf16),
            pltpu.VMEM((R - 4, C - 32, CH), bf16),
            pltpu.VMEM((4, R, CH), bf16),
            pltpu.VMEM((NF, 4, R, CH), bf16),
            pltpu.VMEM((2, 2, C, CH), bf16),
            pltpu.VMEM((NH, 2, PIECE, CH), bf16),
            pltpu.VMEM((NH // 4, 16, CH), bf16),
            pltpu.VMEM((2, NH // 4, 16, CH), bf16),
            pltpu.VMEM((NH, 2, PIECE, CH), bf16),
            pltpu.VMEM((4, R, CH), bf16),
            pltpu.VMEM((2, 4, R, CH), bf16),
            pltpu.VMEM((4, STRIP, CH), f32),
            pltpu.VMEM((4, STRIP, CH), f32),
            pltpu.VMEM((4, SOUT, CH), f32),
            dma((7,)), dma((1,)), dma((1,)), dma((NF,)), dma((NF,)), dma((NF,)), dma((2,)), dma((2,)),
            dma((NF,)), dma((NH,)), dma((NH,)), dma((2,)), dma((NH,)), dma((NF,)),
            dma((2,)), dma((2,)),
        ],
        compiler_params=pltpu.CompilerParams(
            collective_id=0, has_side_effects=True, vmem_limit_bytes=56 << 20
        ),
        cost_estimate=pl.CostEstimate(
            flops=3_500_000_000, bytes_accessed=3_000_000, transcendentals=2_600_000
        ),
    )(
        jnp.transpose(adjacency, (0, 2, 1)), jnp.transpose(edge_flips), state_field,
        conv_first.reshape(9 * CH, CH), bias_first.reshape(1, CH),
        conv_second.reshape(9 * CH, CH), bias_second.reshape(1, CH),
        norm_gain.reshape(1, CH), up_weight, up_bias.reshape(1, -1),
        down_weight, down_bias.reshape(1, CH),
    )


def solution(mesh):
    in_specs = (P("face", "row", None, None), P(), P(), P(), P(), P(), P(), P(), P(), P(), P(), P())
    out_specs = P("face", "row", None, None)
    return jax.shard_map(
        per_device, mesh=mesh, in_specs=in_specs, out_specs=out_specs, check_vma=False
    )
```

```python
import jax
import jax.numpy as jnp
from jax import lax
from jax.experimental import pallas as pl
from jax.experimental.pallas import tpu as pltpu
from jax.sharding import PartitionSpec as P

MESH = pl.DeviceIdType.MESH
bf16 = jnp.bfloat16
f32 = jnp.float32

NF = 8
NR = 16
R = 16
C = 256
CH = 128
K3 = 3 * CH
NH = 2 * NF
PIECE = C // NF
STRIP = 32
SOUT = 24


def dot(a, b):
    return jnp.dot(a, b, preferred_element_type=f32)


def gelu(v):
    return (0.5 * v) * (1.0 + lax.erf(v * 0.7071067811865476))


def put3(ref, row, v):
    zero = jnp.zeros((1, CH), bf16)
    ref[row, :, 0:CH] = jnp.concatenate([zero, v[:-1]], 0)
    ref[row, :, CH : 2 * CH] = v
    ref[row, :, 2 * CH : K3] = jnp.concatenate([v[1:], zero], 0)


def kernel(
    adj, flips, x_hbm, w1_hbm, b1, w2_hbm, b2, gain, wu_hbm, bu, wd_hbm, bd,
    out,
    x, wp1, wp2, wu, wd, X3, F3, T3, NS, P15, COL, HIN, PB, CT, CTB, ST, SEL, SIN, EXT, XC, FS,
    locS, viaS, viaR, relS, colS, colR, rowS, rowR, pbS, pbR, ctS, ctR, stS, stR, selS, selR,
):
    f = lax.axis_index("face")
    r = lax.axis_index("row")
    top = r == 0
    bottom = r == NR - 1
    hot = jnp.logical_or(top, bottom)
    middle = r == 1
    here = (f + 3) % NF
    relay = r == NR - 2
    re = jnp.where(bottom, 1, 0)
    h = 2 * f + re
    place = f % 4

    def hot_device(m):
        return {"face": m // 2, "row": (m % 2) * (NR - 1)}

    local = [
        pltpu.make_async_copy(src, dst, locS.at[i])
        for i, (src, dst) in enumerate(
            (
                (x_hbm.at[0], x),
                (w1_hbm, wp1.at[pl.ds(0, 3 * K3), pl.ds(0, CH)]),
                (w1_hbm, wp1.at[pl.ds(K3, 3 * K3), pl.ds(CH, CH)]),
                (w2_hbm, wp2.at[pl.ds(0, 3 * K3), pl.ds(0, CH)]),
                (w2_hbm, wp2.at[pl.ds(K3, 3 * K3), pl.ds(CH, CH)]),
                (wu_hbm, wu),
                (wd_hbm, wd),
            )
        )
    ]
    for copy in local:
        copy.start()

    barrier = pltpu.get_barrier_semaphore()

    def greet(device):
        pl.semaphore_signal(barrier, inc=1, device_id=device, device_id_type=MESH)

    @pl.when(middle)
    def _():
        @pl.loop(0, NF)
        def _(o):
            greet({"face": o, "row": NR - 1})

        @pl.loop(0, NF)
        def _(o):
            greet({"face": o, "row": 0})

    @pl.loop(1, NF)
    def _(o):
        greet({"face": (f + o) % NF, "row": jnp.where(bottom, NR - 2, r)})

    @pl.when(r > 0)
    def _():
        greet({"face": f, "row": r - 1})

    @pl.when(r < NR - 1)
    def _():
        greet({"face": f, "row": r + 1})

    def col_copy(o, slot):
        return pltpu.make_async_remote_copy(
            src_ref=COL.at[slot], dst_ref=COL.at[slot],
            send_sem=colS.at[o], recv_sem=colR.at[slot],
            device_id={"face": (f + o) % NF, "row": r}, device_id_type=MESH,
        )

    def row_copy(d):
        return pltpu.make_async_remote_copy(
            src_ref=x_hbm.at[0, pl.ds((1 - d) * (R - 2), 2)], dst_ref=HIN.at[d],
            send_sem=rowS.at[d], recv_sem=rowR.at[d],
            device_id={"face": f, "row": r + 1 - 2 * d}, device_id_type=MESH,
        )

    def piece_copy(m, slot):
        return pltpu.make_async_remote_copy(
            src_ref=x_hbm.at[
                0, pl.ds(re * (R - 2), 2), pl.ds(pl.multiple_of(m * PIECE, PIECE), PIECE)
            ],
            dst_ref=PB.at[slot],
            send_sem=pbS.at[m], recv_sem=pbR.at[slot],
            device_id={"face": (m + NF - 3) % NF, "row": 1}, device_id_type=MESH,
        )

    def to_relay():
        return pltpu.make_async_remote_copy(
            src_ref=COL.at[f], dst_ref=P15, send_sem=viaS.at[0], recv_sem=viaR.at[0],
            device_id={"face": f, "row": NR - 2}, device_id_type=MESH,
        )

    def relay_copy(o):
        return pltpu.make_async_remote_copy(
            src_ref=P15, dst_ref=COL.at[f], send_sem=relS.at[o], recv_sem=colR.at[f],
            device_id={"face": (f + o) % NF, "row": NR - 1}, device_id_type=MESH,
        )

    def send_end_row():
        @pl.loop(0, NF)
        def _(o):
            piece_copy((f + o) % NF, h).start()

    def send_first():
        busy = jnp.logical_or(top, relay)

        @pl.when(busy)
        def _():
            pl.semaphore_wait(barrier, 2 * NF)

        @pl.when(jnp.logical_not(busy))
        def _():
            pl.semaphore_wait(barrier, NF + 1)

        @pl.loop(1, NF)
        def _(o):
            col_copy(o, f).start()

        @pl.when(top)
        def _():
            send_end_row()

        row_copy(0).start()

        @pl.when(r > 0)
        def _():
            row_copy(1).start()

        @pl.when(relay)
        def _():
            to_relay().wait_recv()

            @pl.loop(1, NF)
            def _(o):
                relay_copy(o).start()

    @pl.when(bottom)
    def _():
        pl.semaphore_wait(barrier, NF + 1)
        send_end_row()
        row_copy(1).start()

    zero = jnp.zeros((K3, CH), bf16)
    for ref in (wp1, wp2):
        ref[3 * K3 : 4 * K3, 0:CH] = zero
        ref[0:K3, CH : 2 * CH] = zero
    bias1 = b1[...]
    bias2 = b2[...]
    norm_gain = gain[...]
    bias_up = bu[...]
    bias_down = bd[...]
    local[0].wait()

    def column(c):
        base = (c // 16) * 16
        rows = [x[i, base : base + 16, :].astype(f32)[c - base : c - base + 1] for i in range(R)]
        return jnp.concatenate(rows, 0)

    for k, c in enumerate((0, 1, C - 2, C - 1)):
        own = column(c)
        COL[f, k] = own.astype(bf16)
        XC[k] = jnp.zeros((STRIP, CH), f32)
        XC[k, 2 : 2 + R, :] = own

    @pl.when(bottom)
    def _():
        to_relay().start()

    def send_at(point):
        @pl.when(jnp.logical_and(jnp.where(place == 3, 0, jnp.where(place == 0, 2, 1)) == point, jnp.logical_not(bottom)))
        def _():
            send_first()

    send_at(0)

    @pl.loop(0, R)
    def _(i):
        put3(X3, i + 2, x[i])

    def conv1_pairs(starts):
        lhs = jnp.concatenate(
            [jnp.concatenate([X3[k + t] for t in range(4)], 1) for k in starts], 0
        )
        y = dot(lhs, wp1[...])
        for q, k in enumerate(starts):
            for j in range(2):
                v = y[C * q : C * (q + 1), CH * j : CH * (j + 1)]
                put3(F3, k + j, gelu(v + bias1).astype(bf16))

    local[1].wait()
    local[2].wait()
    conv1_pairs((2,))
    send_at(1)

    @pl.loop(0, 2)
    def _(g):
        conv1_pairs([4 + 6 * g + 2 * i for i in range(3)])

    send_at(2)

    for copy in local[3:]:
        copy.wait()

    def conv2_norm(segments):
        lhs = jnp.concatenate(
            [jnp.concatenate([F3[k + t, a:b, :] for t in range(4)], 1) for k, a, b in segments], 0
        )
        y = dot(lhs, wp2[...])
        parts, at = [], 0
        for k, a, b in segments:
            parts += [y[at : at + b - a, CH * j : CH * (j + 1)] for j in range(2)]
            at += b - a
        second = jnp.concatenate(parts, 0) + bias2
        second = second - jnp.mean(second, -1, keepdims=True)
        spread = jnp.mean(second * second, -1, keepdims=True)
        return (second * lax.rsqrt(spread + 1e-6) * norm_gain).astype(bf16)

    def pointwise(normed, skip):
        hidden = gelu(dot(normed, wu[...]) + bias_up).astype(bf16)
        return (skip.astype(f32) + (dot(hidden, wd[...]) + bias_down)).astype(bf16)

    def finish(segments):
        cells = [(k + j, a, b) for k, a, b in segments for j in range(2)]
        skip = jnp.concatenate([x[k, a:b, :] for k, a, b in cells], 0)
        mixed, at = pointwise(conv2_norm(segments), skip), 0
        for k, a, b in cells:
            out[0, k, a:b, :] = mixed[at : at + b - a]
            at += b - a

    fl, el = adj[0, 2, f], adj[1, 2, f] % 2
    fr, er = adj[0, 3, f], adj[1, 3, f] % 2

    def sel_copy(d):
        return pltpu.make_async_remote_copy(
            src_ref=SEL, dst_ref=SIN.at[d],
            send_sem=selS.at[d], recv_sem=selR.at[d],
            device_id={"face": f, "row": r + 1 - 2 * d}, device_id_type=MESH,
        )

    def send_strips():
        @pl.loop(1, NF)
        def _(o):
            col_copy(o, (f + NF - o) % NF).wait_recv()

        SEL[0] = COL[fl, 3 * el]
        SEL[1] = COL[fl, 1 + el]
        SEL[2] = COL[fr, 3 * er]
        SEL[3] = COL[fr, 1 + er]

        @pl.when(r < NR - 1)
        def _():
            sel_copy(0).start()

        @pl.when(r > 0)
        def _():
            sel_copy(1).start()

    def chosen_copy(m, slot):
        return pltpu.make_async_remote_copy(
            src_ref=ST.at[m],
            dst_ref=HIN.at[m % 2, pl.ds(0, 2), pl.ds(pl.multiple_of(slot * PIECE, PIECE), PIECE)],
            send_sem=stS.at[m], recv_sem=stR.at[slot],
            device_id=hot_device(m), device_id_type=MESH,
        )

    def corner_copy(m, side):
        return pltpu.make_async_remote_copy(
            src_ref=CT, dst_ref=CTB.at[side],
            send_sem=ctS.at[m], recv_sem=ctR.at[side],
            device_id=hot_device(m), device_id_type=MESH,
        )

    has_corner = jnp.logical_or(here == 0, here == NF - 1)
    side = jnp.where(here == 0, 0, 1)

    def order_of(o):
        return 2 * (o % NF) + o // NF

    def send_pieces():
        @pl.loop(0, NH)
        def _(m):
            pltpu.make_async_remote_copy(
                src_ref=ST.at[m], dst_ref=PB.at[m], send_sem=stS.at[m], recv_sem=pbR.at[m],
                device_id=hot_device(m), device_id_type=MESH,
            ).wait_recv()

        @pl.when(has_corner)
        def _():
            for g in range(NH // 4):
                cells = []
                for e in range(4 * g, 4 * g + 4):
                    for j in range(2):
                        first = PB[e, j, 0:16, :].astype(f32)[0:2]
                        last = PB[e, j, PIECE - 16 : PIECE, :].astype(f32)[14:16]
                        cells.append(jnp.where(side == 0, first, last))
                CT[g] = jnp.concatenate(cells, 0).astype(bf16)

        @pl.loop(0, NH)
        def _(o):
            m = order_of(o)
            ST[m] = PB[2 * adj[0, m % 2, m // 2] + adj[1, m % 2, m // 2]]
            chosen_copy(m, here).start()

            @pl.when(has_corner)
            def _():
                corner_copy(m, side).start()

    inner = C - 32
    half = R // 2 - 2

    @pl.loop(0, 2)
    def _(g):
        normed = conv2_norm([(2 + half * g + 2 * i, 16, C - 16) for i in range(half // 2)])
        for i in range(half):
            NS[half * g + i] = normed[inner * i : inner * (i + 1)]

    send_strips()

    @pl.loop(0, 2)
    def _(g):
        rows = [half * g + i for i in range(half)]
        skip = jnp.concatenate([x[2 + i, 16 : C - 16, :] for i in rows], 0)
        mixed = pointwise(jnp.concatenate([NS[i] for i in rows], 0), skip)
        for q, i in enumerate(rows):
            out[0, 2 + i, 16 : C - 16, :] = mixed[inner * q : inner * (q + 1)]

        @pl.when(jnp.logical_and(middle, jnp.logical_and(f > 0, g == jnp.where(place < 2, 1, 0))))
        def _():
            send_pieces()

    @pl.when(r > 0)
    def _():
        row_copy(0).wait_recv()
        for j in range(2):
            put3(X3, j, HIN[0, j])

    @pl.when(r < NR - 1)
    def _():
        row_copy(1).wait_recv()
        for j in range(2):
            put3(X3, R + 2 + j, HIN[1, j])

    @pl.when(jnp.logical_not(hot))
    def _():
        conv1_pairs((0, R))

    @pl.when(jnp.logical_and(middle, f == 0))
    def _():
        send_pieces()

    @pl.when(jnp.logical_not(hot))
    def _():
        finish([(k, 16, C - 16) for k in (0, R - 2)])

    @pl.when(hot)
    def _():
        conv1_pairs((R * (1 - re),))

    @pl.when(r > 0)
    def _():
        sel_copy(0).wait_recv()

    @pl.when(r < NR - 1)
    def _():
        sel_copy(1).wait_recv()

    for k in range(4):
        EXT[k] = jnp.zeros((STRIP, CH), f32)
        EXT[k, 2 : 2 + R, :] = SEL[k].astype(f32)

    @pl.when(r > 0)
    def _():
        for k in range(4):
            EXT[k, 0:2, :] = SIN[0, k].astype(f32)[R - 2 : R]
        for j in range(2):
            first, last = HIN[0, j, 0:16, :].astype(f32), HIN[0, j, C - 16 : C, :].astype(f32)
            for k, v in enumerate((first[0:1], first[1:2], last[14:15], last[15:16])):
                XC[k, j : j + 1, :] = v

    @pl.when(r < NR - 1)
    def _():
        for k in range(4):
            EXT[k, R + 2 : R + 4, :] = SIN[1, k].astype(f32)[0:2]
        for j in range(2):
            first, last = HIN[1, j, 0:16, :].astype(f32), HIN[1, j, C - 16 : C, :].astype(f32)
            for k, v in enumerate((first[0:1], first[1:2], last[14:15], last[15:16])):
                XC[k, R + 2 + j : R + 3 + j, :] = v

    def patch(ref, row, first, lanes, value, at):
        cells = ref[row, first : first + 16, lanes * CH : (lanes + 1) * CH].astype(f32)
        rows = lax.broadcasted_iota(jnp.int32, (16, CH), 0)
        ref[row, first : first + 16, lanes * CH : (lanes + 1) * CH] = jnp.where(
            rows == at, value, cells
        ).astype(bf16)

    def taps(columns):
        return jnp.concatenate([v[a : a + v.shape[0] - 2] for a in range(3) for v in columns], 1)

    def outer_left(l0, l1, x0):
        return taps((jnp.where(el == 1, l1, x0), l0, jnp.where(el == 1, x0, l1)))

    def outer_right(r0, r1, x3):
        return taps((jnp.where(er == 1, r1, x3), r0, jnp.where(er == 1, x3, r1)))

    count = SOUT + 2
    lhs = jnp.concatenate(
        [
            outer_left(EXT[0, 0:count], EXT[1, 0:count], XC[0, 0:count]),
            taps((EXT[0, 0:count], XC[0, 0:count], XC[1, 0:count])),
            taps((XC[2, 0:count], XC[3, 0:count], EXT[2, 0:count])),
            outer_right(EXT[2, 0:count], EXT[3, 0:count], XC[3, 0:count]),
        ],
        0,
    )
    strips = gelu(dot(lhs.astype(bf16), wp1[0 : 3 * K3, 0:CH]) + bias1)
    for k in range(4):
        FS[k] = strips[SOUT * k : SOUT * (k + 1)]

    edge_row = lax.broadcasted_iota(jnp.int32, (16, 2 * CH), 0)
    first_half = lax.broadcasted_iota(jnp.int32, (16, 2 * CH), 1) < CH

    @pl.loop(0, R + 2)
    def _(k):
        v = [FS[i, pl.ds(k, 1), :] for i in range(4)]
        cells = F3[k, 0:16, 0 : 2 * CH].astype(f32)
        cells = jnp.where(edge_row == 0, jnp.concatenate([v[0], v[1]], 1), cells)
        beside = jnp.logical_and(edge_row == 1, first_half)
        cells = jnp.where(beside, jnp.concatenate([v[1], v[1]], 1), cells)
        F3[k, 0:16, 0 : 2 * CH] = cells.astype(bf16)
        cells = F3[k, C - 16 : C, CH:K3].astype(f32)
        cells = jnp.where(edge_row == 15, jnp.concatenate([v[2], v[3]], 1), cells)
        beside = jnp.logical_and(edge_row == 14, jnp.logical_not(first_half))
        cells = jnp.where(beside, jnp.concatenate([v[2], v[2]], 1), cells)
        F3[k, C - 16 : C, CH:K3] = cells.astype(bf16)

    @pl.when(jnp.logical_not(hot))
    def _():
        finish([(k, a, a + 16) for k in range(0, R, 2) for a in (0, C - 16)])

    @pl.when(hot)
    def _():
        outer = [(k, a, a + 16) for k in range(2, R - 2, 2) for a in (0, C - 16)]
        finish([((R - 2) * (1 - re), 0, C)] + outer)

    def corner_cell(face, edge, j, at):
        e = 2 * face + edge
        tile = CTB[at // 2, e // 4].astype(f32)
        rows = lax.broadcasted_iota(jnp.int32, tile.shape, 0)
        return jnp.sum(
            jnp.where(rows == 4 * (e % 4) + 2 * j + at % 2, tile, 0.0), 0, keepdims=True
        )

    @pl.when(hot)
    def _():
        s = re

        @pl.loop(0, NF)
        def _(m):
            chosen_copy(h, m).wait_recv()

        for d in range(2):
            corner_copy(h, d).wait_recv()

        fu, eu = adj[0, s, f], adj[1, s, f]
        flip = flips[s, f]
        rows = lax.broadcasted_iota(jnp.int32, (C, C), 0)
        cols = lax.broadcasted_iota(jnp.int32, (C, C), 1)
        order = jnp.where(cols == jnp.where(flip == 1, C - 1 - rows, rows), 1.0, 0.0).astype(bf16)
        near = HIN[s, 0].astype(f32), HIN[s, 1].astype(f32)
        edge = jnp.where(eu == 1, near[1], near[0]).astype(bf16)
        turned = dot(order, jnp.concatenate([x[(R - 1) * s], edge], 1))
        mine = turned[:, 0:CH]
        put3(X3, 1 + (R + 1) * s, turned[:, CH : 2 * CH].astype(bf16))
        for t, v in enumerate(
            (
                jnp.where(eu == 1, near[0], mine),
                jnp.where(eu == 1, near[1], near[0]),
                jnp.where(eu == 1, mine, near[1]),
            )
        ):
            put3(T3, t, v.astype(bf16))
        none = jnp.zeros((1, CH), f32)
        for e in range(2):
            g, ge = adj[0, 2 + e, fu], adj[1, 2 + e, fu] % 2
            cells = [corner_cell(g, eu, j, 3 * ge) for j in range(2)]
            rim = (
                jnp.where(eu == 1, cells[0], none),
                jnp.where(eu == 1, cells[1], cells[0]),
                jnp.where(eu == 1, none, cells[1]),
            )
            for t in range(3):
                patch(T3, t, (C - 16) * e, 2 * e, rim[t], 15 * e)
            g0, e0 = adj[0, 2 + e, f], adj[1, 2 + e, f] % 2
            g, ge, turn = adj[0, s, g0], adj[1, s, g0], flips[s, g0]
            for depth in range(2):
                at = 3 * e0 if depth == 0 else 1 + e0
                at = jnp.where(turn == 1, 3 - at, at)
                EXT[2 * e + depth, pl.ds(1 + (R + 1) * s, 1), :] = corner_cell(g, ge, ge, at)

        for t in range(2):
            k = 2 + (R - 2) * s + t
            patch(X3, k, 0, 0, EXT[0, pl.ds(k, 1), :], 0)
            patch(X3, k, C - 16, 2, EXT[2, pl.ds(k, 1), :], 15)

        near_rows = pl.ds(1 + (R - 1) * s, 10)
        strip = jnp.concatenate(
            [
                outer_left(EXT[0, near_rows], EXT[1, near_rows], XC[0, near_rows]),
                outer_right(EXT[2, near_rows], EXT[3, near_rows], XC[3, near_rows]),
            ],
            0,
        ).astype(bf16)
        lhs = jnp.concatenate(
            [
                jnp.concatenate([T3[t] for t in range(3)], 1),
                jnp.concatenate([X3[1 + (R - 1) * s + t] for t in range(3)], 1),
                strip,
            ],
            0,
        )
        y = gelu(dot(lhs, wp1[0 : 3 * K3, 0:CH]) + bias1)
        put3(F3, (R + 1) * s, dot(order, y[0:C].astype(bf16)).astype(bf16))
        put3(F3, 1 + (R - 1) * s, y[C : 2 * C].astype(bf16))
        patch(F3, 1 + (R - 1) * s, 0, 0, y[2 * C : 2 * C + 1], 0)
        patch(F3, 1 + (R - 1) * s, C - 16, 2, y[2 * C + 8 : 2 * C + 9], 15)
        finish([((R - 2) * s, 0, C)])

    @pl.when(jnp.logical_not(bottom))
    def _():
        @pl.loop(1, NF)
        def _(o):
            col_copy(o, f).wait_send()

        row_copy(0).wait_send()
        sel_copy(0).wait_send()

    @pl.when(r > 0)
    def _():
        row_copy(1).wait_send()
        sel_copy(1).wait_send()

    @pl.when(hot)
    def _():
        @pl.loop(0, NF)
        def _(m):
            piece_copy(m, h).wait_send()

    @pl.when(bottom)
    def _():
        to_relay().wait_send()

    @pl.when(relay)
    def _():
        @pl.loop(1, NF)
        def _(o):
            relay_copy(o).wait_send()

    @pl.when(middle)
    def _():
        @pl.loop(0, NH)
        def _(m):
            chosen_copy(m, here).wait_send()

            @pl.when(has_corner)
            def _():
                corner_copy(m, side).wait_send()


def per_device(
    state_field, adjacency, edge_flips, conv_first, bias_first, conv_second, bias_second,
    norm_gain, up_weight, up_bias, down_weight, down_bias,
):
    vmem = pl.BlockSpec(memory_space=pltpu.VMEM)
    smem = pl.BlockSpec(memory_space=pltpu.SMEM)
    hbm = pl.BlockSpec(memory_space=pl.ANY)
    dma = pltpu.SemaphoreType.DMA
    return pl.pallas_call(
        kernel,
        out_shape=pltpu.VMEM((1, R, C, CH), bf16),
        in_specs=[smem, smem, hbm, hbm, vmem, hbm, vmem, vmem, hbm, vmem, hbm, vmem],
        out_specs=vmem,
        scratch_shapes=[
            pltpu.VMEM((R, C, CH), bf16),
            pltpu.VMEM((4 * K3, 2 * CH), bf16),
            pltpu.VMEM((4 * K3, 2 * CH), bf16),
            pltpu.VMEM(up_weight.shape, bf16),
            pltpu.VMEM(down_weight.shape, bf16),
            pltpu.VMEM((R + 4, C, K3), bf16),
            pltpu.VMEM((R + 2, C, K3), bf16),
            pltpu.VMEM((3, C, K3), bf16),
            pltpu.VMEM((R - 4, C - 32, CH), bf16),
            pltpu.VMEM((4, R, CH), bf16),
            pltpu.VMEM((NF, 4, R, CH), bf16),
            pltpu.VMEM((2, 2, C, CH), bf16),
            pltpu.VMEM((NH, 2, PIECE, CH), bf16),
            pltpu.VMEM((NH // 4, 16, CH), bf16),
            pltpu.VMEM((2, NH // 4, 16, CH), bf16),
            pltpu.VMEM((NH, 2, PIECE, CH), bf16),
            pltpu.VMEM((4, R, CH), bf16),
            pltpu.VMEM((2, 4, R, CH), bf16),
            pltpu.VMEM((4, STRIP, CH), f32),
            pltpu.VMEM((4, STRIP, CH), f32),
            pltpu.VMEM((4, SOUT, CH), f32),
            dma((7,)), dma((1,)), dma((1,)), dma((NF,)), dma((NF,)), dma((NF,)), dma((2,)), dma((2,)),
            dma((NF,)), dma((NH,)), dma((NH,)), dma((2,)), dma((NH,)), dma((NF,)),
            dma((2,)), dma((2,)),
        ],
        compiler_params=pltpu.CompilerParams(
            collective_id=0, has_side_effects=True, vmem_limit_bytes=56 << 20
        ),
        cost_estimate=pl.CostEstimate(
            flops=3_500_000_000, bytes_accessed=3_000_000, transcendentals=2_600_000
        ),
    )(
        jnp.transpose(adjacency, (0, 2, 1)), jnp.transpose(edge_flips), state_field,
        conv_first.reshape(9 * CH, CH), bias_first.reshape(1, CH),
        conv_second.reshape(9 * CH, CH), bias_second.reshape(1, CH),
        norm_gain.reshape(1, CH), up_weight, up_bias.reshape(1, -1),
        down_weight, down_bias.reshape(1, CH),
    )


def solution(mesh):
    in_specs = (P("face", "row", None, None), P(), P(), P(), P(), P(), P(), P(), P(), P(), P(), P())
    out_specs = P("face", "row", None, None)
    return jax.shard_map(
        per_device, mesh=mesh, in_specs=in_specs, out_specs=out_specs, check_vma=False
    )
```
